32 devices in a mesh: copies: 2 (over y), leaf: 4 (over z), sub: 4 (over x, core).
Axes of the slice: x: 2, y: 2, z: 4, core: 2. Of those that a mesh axis runs over, the one named last changes fastest.
Arguments:
- vectors: bfloat16 [512, 16, 128], P(('copies', 'leaf', 'sub')), parts along dimension 0, may hold values from -6 to 6
- leaf_basis: bfloat16 [512, 64, 128], P(('copies', 'leaf', 'sub')), parts along dimension 0, may hold values from -0.5 to 0.5
- near_blocks: bfloat16 [512, 6, 128, 128], P(('copies', 'leaf', 'sub')), parts along dimension 0, may hold values from -0.21875 to 0.21875
- near_list: int32 [256, 6], P(('leaf', 'sub')), may hold values from 0 to 255, as said below
- near_mask: int32 [256, 6], P(('leaf', 'sub')), may hold values from 0 to 1, as said below
- transfer_low: bfloat16 [960, 64, 64], P(('copies', 'leaf', 'sub')), parts along dimension 0, may hold values from -0.625 to 0.625
- coupling_low: bfloat16 [992, 3, 64, 64], P(('copies', 'leaf', 'sub')), parts along dimension 0, may hold values from -0.21875 to 0.21875
- far_list: int32 [496, 3], P(('leaf', 'sub')), may hold values from 0 to 255, as said below
- far_mask: int32 [496, 3], P(('leaf', 'sub')), may hold values from 0 to 1, as said below
- transfer_top: bfloat16 [60, 64, 64], P('copies'), parts along dimension 0, may hold values from -0.625 to 0.625
- coupling_top: bfloat16 [28, 3, 64, 64], P('copies'), parts along dimension 0, may hold values from -0.21875 to 0.21875
Outputs:
- product: bfloat16 [512, 16, 128], P(('copies', 'leaf', 'sub')), parts along dimension 0
The draws below stay inside these ranges and needn't reach their ends.
There are 2 independent parts, one for each index of `copies`. The reference program is written for one: setup_inputs(seed, part) draws one part's arguments, and reference() takes and returns one part's arrays. A program takes and returns all parts, laid end to end along the dimension named above; an argument that names none is the same for every part. Nothing has to cross between parts.
Inputs may be any that keep to these rules, and one draw needn't show every extreme that they name: `near_list`: slots 0, 1, 2 of row i hold i - 1, i, i + 1 where those leaves exist; slots 3 and up in use hold, first and in any order, those candidates of leaf i that far_list does not couple at level 0; unused slots hold i; on every device some leaf uses all 6 slots. `near_mask`: 1 where the slot of near_list is in use. `far_list`: the slots in use of box t come first and hold candidates of t in its level, in any order; at levels 1 and up every candidate of t is in use; at level 0 every candidate of a leaf is either in use here or in near_list, never both; unused slots hold t. `far_mask`: 1 where the slot of far_list is in use; on every device some leaf uses all 3 slots.
All inputs are finite; a program needn't handle non-finite values.
Results may differ from the reference program's by a relative error of at most 0.0004.
Values may be sent and summed in bfloat16 or wider, within the bound.
A program may use at most 128 MiB of HBM per device.

```python
import jax
import jax.numpy as jnp
from jax import lax

PTS = 128
BASIS_RANK_SIZE = 64
VECTOR_COUNT = 16
K_NEAR = 6
K_FAR = 3
LEAF_DEV = 16
TREE_DEVS = 16
LEAVES = 256
BOX_DEV = 31
LOW_LEVELS = 5
TOP_LEVELS = 4


def candidate_boxes(box_total):
    target = jnp.arange(box_total, dtype=jnp.int32)[:, None]
    step_table = jnp.where(target % 2 == 0, jnp.array([[-2, 2, 3]], jnp.int32), jnp.array([[-3, -2, 2]], jnp.int32))
    source = target + step_table
    inside = (source >= 0) & (source < box_total)
    return (target, source, inside)


def compact_slots(key, target, source, in_use):
    slots = source.shape[1]
    score_value = jax.random.randint(key, source.shape, 0, 1 << 20) * slots + jnp.arange(slots, dtype=jnp.int32)[None, :]
    score_value = jnp.where(in_use, score_value, score_value + (1 << 28))
    ranking = jnp.argsort(score_value, axis=1, stable=True)
    picked = jnp.take_along_axis(source, ranking, axis=1)
    used_slot = jnp.take_along_axis(in_use, ranking, axis=1)
    return (jnp.where(used_slot, picked, target), used_slot.astype(jnp.int32))


def leaf_choice(key):
    target, source, inside = candidate_boxes(LEAVES)
    coin_flip = jax.random.randint(jax.random.fold_in(key, 1), (LEAVES, 3), 0, 2) == 1
    near_full = jax.random.randint(jax.random.fold_in(key, 2), (TREE_DEVS,), 3, LEAF_DEV - 3)
    far_full = 3 + (near_full - 3 + 1 + jax.random.randint(jax.random.fold_in(key, 3), (TREE_DEVS,), 0, LEAF_DEV - 7)) % (LEAF_DEV - 6)
    position = jnp.arange(LEAF_DEV, dtype=jnp.int32)[None, :]
    all_near = (position == near_full[:, None]).reshape(LEAVES, 1)
    all_far = (position == far_full[:, None]).reshape(LEAVES, 1)
    far_pick = jnp.where(all_far, True, jnp.where(all_near, False, coin_flip)) & inside
    near_pick = inside & jnp.logical_not(far_pick)
    return (target, source, far_pick, near_pick)


def near_slots(key, own_key):
    target, source, far_pick, near_pick = leaf_choice(key)
    fixed = target + jnp.arange(-1, 2, dtype=jnp.int32)[None, :]
    fixed_ok = (fixed >= 0) & (fixed < LEAVES)
    fixed = jnp.where(fixed_ok, fixed, target)
    extra, extra_use = compact_slots(own_key, target, source, near_pick)
    return (jnp.concatenate([fixed, extra], 1), jnp.concatenate([fixed_ok.astype(jnp.int32), extra_use], 1))


def far_slots(key, own_key):
    target, source, far_pick, near_pick = leaf_choice(key)
    listed_parts = []
    used_parts = []
    for height in range(LOW_LEVELS):
        per_dev = LEAF_DEV >> height
        if height == 0:
            level_target, level_source, level_use = (target, source, far_pick)
        else:
            level_target, level_source, level_use = candidate_boxes(per_dev * TREE_DEVS)
        listed, in_use = compact_slots(jax.random.fold_in(own_key, height), level_target, level_source, level_use)
        listed_parts.append(listed.reshape(TREE_DEVS, per_dev, K_FAR))
        used_parts.append(in_use.reshape(TREE_DEVS, per_dev, K_FAR))
    listed = jnp.concatenate(listed_parts, 1).reshape(-1, K_FAR)
    in_use = jnp.concatenate(used_parts, 1).reshape(-1, K_FAR)
    return (listed, in_use)


def draw_near_list(key, part):
    own_key = jax.random.fold_in(key, 5)
    listed, in_use = near_slots(key, own_key)
    return listed


def draw_near_mask(key, part):
    own_key = jax.random.fold_in(key, 6)
    listed, in_use = near_slots(key, own_key)
    return in_use


def draw_far_list(key, part):
    own_key = jax.random.fold_in(key, 7)
    listed, in_use = far_slots(key, own_key)
    return listed


def draw_far_mask(key, part):
    own_key = jax.random.fold_in(key, 8)
    listed, in_use = far_slots(key, own_key)
    return in_use


def block_levels(key, shape, split, low, top_value):
    factor_of = 1.0
    for axis_at, shards_of in split:
        draws = jax.random.uniform(jax.random.fold_in(jax.random.fold_in(key, 6), axis_at), (shards_of,), jnp.float32, low / len(split), top_value / len(split))
        factor_of = factor_of * jnp.repeat(jnp.exp(draws), shape[axis_at] // shards_of).reshape((-1,) + (1,) * (len(shape) - 1 - axis_at))
    return factor_of


def bell_draw(stream_key, dims, scale, bound, shards=(), kind=jnp.bfloat16):
    loudness = block_levels(stream_key, dims, shards, -0.22, 0.18) if shards else 1.0
    result = jax.random.normal(stream_key, dims, jnp.float32) * scale * loudness
    return jnp.minimum(jnp.maximum(result, -bound), bound).astype(kind)


def setup_inputs(seed: int = 0, part: int = 0) -> dict:
    splits = jax.random.split(jax.random.key(seed), 12)
    part_splits = jax.random.split(jax.random.fold_in(splits[11], part), 12)
    return {
        "vectors": bell_draw(part_splits[0], (LEAVES, VECTOR_COUNT, PTS), 1.0, 6.0, ((0, 16),)),
        "leaf_basis": bell_draw(part_splits[1], (LEAVES, BASIS_RANK_SIZE, PTS), PTS ** -0.5, 0.5, ((0, 16),)),
        "near_blocks": bell_draw(part_splits[2], (LEAVES, K_NEAR, PTS, PTS), (PTS * K_NEAR) ** -0.5, 0.21875, ((0, 16),)),
        "near_list": draw_near_list(jax.random.fold_in(splits[11], 71), part),
        "near_mask": draw_near_mask(jax.random.fold_in(splits[11], 71), part),
        "transfer_low": bell_draw(part_splits[5], (TREE_DEVS * (2 * LEAF_DEV - 2), BASIS_RANK_SIZE, BASIS_RANK_SIZE), (1.41421356 * BASIS_RANK_SIZE) ** -0.5, 0.625, ((0, 16),)),
        "coupling_low": bell_draw(part_splits[6], (TREE_DEVS * BOX_DEV, K_FAR, BASIS_RANK_SIZE, BASIS_RANK_SIZE), (4 * BASIS_RANK_SIZE * K_FAR) ** -0.5, 0.21875, ((0, 16),)),
        "far_list": draw_far_list(jax.random.fold_in(splits[11], 71), part),
        "far_mask": draw_far_mask(jax.random.fold_in(splits[11], 71), part),
        "transfer_top": bell_draw(part_splits[9], (2 * TREE_DEVS - 2, BASIS_RANK_SIZE, BASIS_RANK_SIZE), (1.41421356 * BASIS_RANK_SIZE) ** -0.5, 0.625),
        "coupling_top": bell_draw(part_splits[10], (TREE_DEVS - 2, K_FAR, BASIS_RANK_SIZE, BASIS_RANK_SIZE), (4 * BASIS_RANK_SIZE * K_FAR) ** -0.5, 0.21875),
    }


def reference(vectors, leaf_basis, near_blocks, near_list, near_mask, transfer_low, coupling_low, far_list, far_mask, transfer_top, coupling_top):
    highest_level = lax.Precision.HIGHEST
    per_dev = LEAF_DEV
    tree_devs = TREE_DEVS
    coefficient = jnp.einsum("ivp,irp->ivr", vectors.astype(jnp.float32), leaf_basis.astype(jnp.float32), precision=highest_level)
    low_mats = transfer_low.reshape(tree_devs, 2 * per_dev - 2, BASIS_RANK_SIZE, BASIS_RANK_SIZE)
    couple_mats = coupling_low.reshape(tree_devs, 2 * per_dev - 1, K_FAR, BASIS_RANK_SIZE, BASIS_RANK_SIZE)
    far_rows = far_list.reshape(tree_devs, 2 * per_dev - 1, K_FAR)
    far_used = far_mask.reshape(tree_devs, 2 * per_dev - 1, K_FAR)
    transfers = []
    offset = 0
    for height in range(LOW_LEVELS - 1):
        box_count = per_dev >> height
        transfers.append(low_mats[:, offset:offset + box_count].reshape(tree_devs * box_count, BASIS_RANK_SIZE, BASIS_RANK_SIZE))
        offset = offset + box_count
    offset = 0
    for height in range(TOP_LEVELS):
        box_count = tree_devs >> height
        transfers.append(transfer_top[offset:offset + box_count])
        offset = offset + box_count
    level_list = [coefficient]
    for height in range(len(transfers)):
        current_level = level_list[-1]
        count_halved = current_level.shape[0] // 2
        matrix_stack = transfers[height].astype(jnp.float32).reshape(count_halved, 2, BASIS_RANK_SIZE, BASIS_RANK_SIZE)
        level_list.append(jnp.einsum("juyz,juza->jya", current_level.reshape(count_halved, 2, VECTOR_COUNT, BASIS_RANK_SIZE), matrix_stack, precision=highest_level))
    far_terms = []
    offset = 0
    for height in range(LOW_LEVELS):
        box_count = per_dev >> height
        partners = far_rows[:, offset:offset + box_count].reshape(-1, K_FAR)
        in_use = far_used[:, offset:offset + box_count].reshape(-1, K_FAR).astype(jnp.float32)
        matrix_stack = couple_mats[:, offset:offset + box_count].reshape(-1, K_FAR, BASIS_RANK_SIZE, BASIS_RANK_SIZE).astype(jnp.float32)
        sources = level_list[height][partners] * in_use[:, :, None, None]
        far_terms.append(jnp.einsum("tkvr,tkrs->tvs", sources, matrix_stack, precision=highest_level))
        offset = offset + box_count
    offset = 0
    for height in range(1, TOP_LEVELS):
        current_level = level_list[LOW_LEVELS - 1 + height]
        box_count = current_level.shape[0]
        matrix_stack = coupling_top[offset:offset + box_count].astype(jnp.float32)
        offset = offset + box_count
        target = jnp.arange(box_count, dtype=jnp.int32)[:, None]
        step_table = jnp.where(target % 2 == 0, jnp.array([[-2, 2, 3]], jnp.int32), jnp.array([[-3, -2, 2]], jnp.int32))
        partners = target + step_table
        inside = ((partners >= 0) & (partners < box_count)).astype(jnp.float32)
        sources = current_level[jnp.clip(partners, 0, box_count - 1)] * inside[:, :, None, None]
        far_terms.append(jnp.einsum("tkvr,tkrs->tvs", sources, matrix_stack, precision=highest_level))
    far_terms.append(jnp.zeros((1, VECTOR_COUNT, BASIS_RANK_SIZE), jnp.float32))
    downward = far_terms[-1]
    for height in range(len(transfers) - 1, -1, -1):
        matrix_stack = transfers[height].astype(jnp.float32)
        spread = jnp.repeat(downward, 2, axis=0)
        downward = far_terms[height] + jnp.einsum("tvs,trs->tvr", spread, matrix_stack, precision=highest_level)
    leaf_term = jnp.einsum("ivr,irp->ivp", downward, leaf_basis.astype(jnp.float32), precision=highest_level)

    def near_group(pieces):
        blocks, partners, in_use = pieces
        sources = vectors[partners].astype(jnp.float32) * in_use[:, :, None, None].astype(jnp.float32)
        return jnp.einsum("ikvp,ikpq->ivq", sources, blocks.astype(jnp.float32), precision=highest_level)

    near_terms = lax.map(near_group, (near_blocks.reshape(tree_devs, per_dev, K_NEAR, PTS, PTS), near_list.reshape(tree_devs, per_dev, K_NEAR), near_mask.reshape(tree_devs, per_dev, K_NEAR)))
    near_terms = near_terms.reshape(tree_devs * per_dev, VECTOR_COUNT, PTS)
    return (near_terms + leaf_term).astype(jnp.bfloat16)
```

```python
import functools

import jax
import jax.numpy as jnp
from jax import lax
from jax.experimental import pallas as pl
from jax.experimental.pallas import tpu as pltpu
from jax.sharding import PartitionSpec as P

RIM = 2
MESH = pl.DeviceIdType.MESH
F32 = jnp.float32
BF16 = jnp.bfloat16


def bdot(left, right, transposed=False):
    contract = 2 if transposed else 1
    return lax.dot_general(
        left, right, (((2,), (contract,)), ((0,), (0,))), preferred_element_type=F32
    )


def split(value):
    high = value.astype(BF16)
    low = (value - high.astype(F32)).astype(BF16)
    return high, low


def stacked(value):
    return jnp.concatenate(split(value), axis=-2)


def folded(value):
    half = value.shape[-2] // 2
    return value[..., :half, :] + value[..., half:, :]


def kernel(
    sizes,
    near_list,
    near_mask,
    far_list,
    far_mask,
    vectors,
    basis,
    near_blocks,
    transfer_low,
    coupling_low,
    transfer_top,
    coupling_top,
    out,
    vec_buf,
    basis_buf,
    near_buf,
    tlow_buf,
    clow_buf,
    ttop_buf,
    ctop_buf,
    near_acc,
    far_acc,
    roots,
    *rest,
):
    leaves, low_levels, tree_devs, num_sub, top_used, k_near, k_far = sizes
    level_bufs = rest[: low_levels - 1]
    top_bufs = rest[low_levels - 1 : low_levels - 1 + top_used]
    local_sem, rim_send, rim_recv, root_send, root_recv = rest[-5:]
    leaf_at = lax.axis_index("leaf")
    device = leaf_at * num_sub + lax.axis_index("sub")
    copy_at = lax.axis_index("copies")

    def place(index):
        return (copy_at, index // num_sub, index % num_sub)

    barrier = pltpu.get_barrier_semaphore()

    def greet(step, carry):
        pl.semaphore_signal(
            barrier, inc=1, device_id=place((device + step) % tree_devs), device_id_type=MESH
        )
        return carry

    lax.fori_loop(1, tree_devs, greet, 0, unroll=tree_devs <= 16)

    moves = [
        (vectors, vec_buf.at[pl.ds(RIM, leaves)]),
        (basis, basis_buf),
        (transfer_low, tlow_buf),
        (near_blocks, near_buf),
        (coupling_low, clow_buf),
        (transfer_top, ttop_buf),
    ]
    for height in range(1, top_used + 1):
        row = tree_devs - 2 * (tree_devs >> height) + device // (1 << height)
        moves.append((coupling_top.at[row], ctop_buf.at[height - 1]))
    copies = [
        pltpu.make_async_copy(source, target, local_sem.at[at])
        for at, (source, target) in enumerate(moves)
    ]
    for copy in copies:
        copy.start()

    starts = [2 * leaves - 2 * (leaves >> height) for height in range(low_levels)]
    counts = [leaves >> height for height in range(low_levels)]
    rims = [min(RIM, count) for count in counts]

    vec_buf[leaves + 2 * RIM] = jnp.zeros(vec_buf.shape[1:], BF16)
    for buf in level_bufs:
        buf[buf.shape[0] - 1] = jnp.zeros(buf.shape[1:], BF16)
    for buf in top_bufs:
        buf[buf.shape[0] - 1] = jnp.zeros(buf.shape[1:], BF16)
    roots[tree_devs] = jnp.zeros(roots.shape[1:], BF16)

    def rim_copies(buf, count, rim, at):
        to_right = pltpu.make_async_remote_copy(
            src_ref=buf.at[pl.ds(count, rim)],
            dst_ref=buf.at[pl.ds(0, rim)],
            send_sem=rim_send.at[2 * at],
            recv_sem=rim_recv.at[2 * at],
            device_id=place(device + 1),
            device_id_type=MESH,
        )
        to_left = pltpu.make_async_remote_copy(
            src_ref=buf.at[pl.ds(rim, rim)],
            dst_ref=buf.at[pl.ds(rim + count, rim)],
            send_sem=rim_send.at[2 * at + 1],
            recv_sem=rim_recv.at[2 * at + 1],
            device_id=place(device - 1),
            device_id_type=MESH,
        )
        return to_right, to_left

    rim_pairs = [rim_copies(vec_buf, leaves, RIM, low_levels - 1)]
    for height in range(low_levels - 1):
        rim_pairs.append(rim_copies(level_bufs[height], counts[height], rims[height], height))

    has_right = device < tree_devs - 1
    has_left = device > 0

    def send_rims(at):
        to_right, to_left = rim_pairs[at]

        @pl.when(has_right)
        def _():
            to_right.start()

        @pl.when(has_left)
        def _():
            to_left.start()

    def take_rims(at):
        to_right, to_left = rim_pairs[at]

        @pl.when(has_left)
        def _():
            to_right.wait_recv()

        @pl.when(has_right)
        def _():
            to_left.wait_recv()

    copies[0].wait()
    copies[1].wait()
    coefs = bdot(vec_buf[pl.ds(RIM, leaves)], basis_buf[...], transposed=True)
    pieces = stacked(coefs)
    level_bufs[0][pl.ds(rims[0], counts[0])] = pieces
    pl.semaphore_wait(barrier, tree_devs - 1)
    send_rims(0)
    send_rims(1)
    copies[2].wait()
    for height in range(1, low_levels):
        below = counts[height - 1]
        moved = folded(bdot(pieces, tlow_buf[pl.ds(starts[height - 1], below)]))
        moved = moved.reshape((below // 2, 2) + moved.shape[1:])
        coefs = moved[:, 0] + moved[:, 1]
        if height < low_levels - 1:
            pieces = stacked(coefs)
            level_bufs[height][pl.ds(rims[height], counts[height])] = pieces
            send_rims(height + 1)
    high, low = split(coefs[0])
    roots[device] = jnp.concatenate([high.astype(F32), low.astype(F32)], axis=-1).astype(BF16)

    def send_root(step, carry):
        pltpu.make_async_remote_copy(
            src_ref=roots.at[device],
            dst_ref=roots.at[device],
            send_sem=root_send,
            recv_sem=root_recv,
            device_id=place((device + step) % tree_devs),
            device_id_type=MESH,
        ).start()
        return carry

    lax.fori_loop(1, tree_devs, send_root, 0, unroll=tree_devs <= 16)

    take_rims(0)
    copies[3].wait()
    near_base = device * leaves - RIM

    def near_step(leaf, carry):
        sources = []
        for slot in range(k_near):
            spot = jnp.where(
                near_mask[leaf, slot] != 0,
                near_list[leaf, slot] - near_base,
                leaves + 2 * RIM,
            )
            sources.append(vec_buf[spot])
        blocks = near_buf[leaf]
        near_acc[leaf] = jnp.dot(
            jnp.concatenate(sources, axis=-1),
            blocks.reshape(blocks.shape[0] * blocks.shape[1], blocks.shape[2]),
            preferred_element_type=F32,
        )
        return carry

    lax.fori_loop(0, leaves, near_step, 0, unroll=True)

    copies[4].wait()
    for height in range(low_levels - 1):
        take_rims(height + 1)
        buf = level_bufs[height]
        far_base = device * counts[height] - rims[height]
        zero_spot = buf.shape[0] - 1

        def far_step(box, carry, buf=buf, far_base=far_base, zero_spot=zero_spot, height=height):
            row = starts[height] + box
            total = None
            for slot in range(k_far):
                spot = jnp.where(
                    far_mask[row, slot] != 0, far_list[row, slot] - far_base, zero_spot
                )
                term = jnp.dot(buf[spot], clow_buf[row, slot], preferred_element_type=F32)
                total = term if total is None else total + term
            far_acc[row] = folded(total)
            return carry

        lax.fori_loop(0, counts[height], far_step, 0, unroll=True)

    for copy in copies[5:]:
        copy.wait()
    arrived = roots.at[pl.ds(0, tree_devs - 1)]
    pltpu.make_async_copy(arrived, arrived, root_recv).wait()

    def doubled(matrix):
        return jnp.concatenate([matrix, matrix], axis=-2)

    pieces = roots[pl.ds(0, tree_devs)]
    for height in range(1, top_used + 1):
        below = tree_devs >> (height - 1)
        first = 2 * tree_devs - 2 * below
        mats = ttop_buf[pl.ds(first, below)]
        moved = bdot(pieces, doubled(mats)) if height == 1 else folded(bdot(pieces, mats))
        moved = moved.reshape((below // 2, 2) + moved.shape[1:])
        pieces = stacked(moved[:, 0] + moved[:, 1])
        top_bufs[height - 1][pl.ds(0, below // 2)] = pieces

    root_row = starts[low_levels - 1]
    downward = None
    for height in range(top_used, -1, -1):
        node = device // (1 << height)
        boxes = tree_devs >> height
        total = None
        if height == 0:
            for slot in range(k_far):
                spot = jnp.where(
                    far_mask[root_row, slot] != 0, far_list[root_row, slot], tree_devs
                )
                term = jnp.dot(
                    roots[spot], doubled(clow_buf[root_row, slot]), preferred_element_type=F32
                )
                total = term if total is None else total + term
        else:
            odd = node % 2
            for slot, (even_step, odd_step) in enumerate(((-2, -3), (2, -2), (3, 2))):
                source = node + jnp.where(odd == 1, odd_step, even_step)
                spot = jnp.where((source >= 0) & (source < boxes), source, boxes)
                term = jnp.dot(
                    top_bufs[height - 1][spot],
                    ctop_buf[height - 1, slot],
                    preferred_element_type=F32,
                )
                total = term if total is None else total + term
            total = folded(total)
        if downward is not None:
            matrix = ttop_buf[2 * tree_devs - 2 * boxes + node]
            total = total + folded(
                lax.dot_general(
                    stacked(downward), matrix, (((1,), (1,)), ((), ())), preferred_element_type=F32
                )
            )
        downward = total

    expanded = downward[None]
    for height in range(low_levels - 2, -1, -1):
        count = counts[height]
        spread = stacked(expanded)
        spread = jnp.broadcast_to(spread[:, None], (count // 2, 2) + spread.shape[1:])
        spread = spread.reshape((count,) + spread.shape[2:])
        mats = tlow_buf[pl.ds(starts[height], count)]
        expanded = far_acc[pl.ds(starts[height], count)] + folded(
            bdot(spread, mats, transposed=True)
        )
    leaf_term = folded(bdot(stacked(expanded), basis_buf[...]))
    out[...] = (near_acc[...] + leaf_term).astype(out.dtype)

    sent = roots.at[pl.ds(0, tree_devs - 1)]
    pltpu.make_async_copy(sent, sent, root_send).wait()
    for to_right, to_left in rim_pairs:

        @pl.when(has_right)
        def _(to_right=to_right):
            to_right.wait_send()

        @pl.when(has_left)
        def _(to_left=to_left):
            to_left.wait_send()


def per_device(
    vectors,
    leaf_basis,
    near_blocks,
    near_list,
    near_mask,
    transfer_low,
    coupling_low,
    far_list,
    far_mask,
    transfer_top,
    coupling_top,
):
    tree_devs = lax.axis_size(("leaf", "sub"))
    num_sub = lax.axis_size("sub")
    leaves, num_vectors, points = vectors.shape
    rank = leaf_basis.shape[1]
    k_near = near_blocks.shape[1]
    k_far = coupling_low.shape[1]
    low_levels = leaves.bit_length()
    top_used = max(tree_devs.bit_length() - 3, 0)
    counts = [leaves >> height for height in range(low_levels - 1)]
    boxes = [
        pltpu.VMEM((count + 2 * min(RIM, count) + 1, 2 * num_vectors, rank), BF16)
        for count in counts
    ] + [
        pltpu.VMEM(((tree_devs >> height) + 1, 2 * num_vectors, rank), BF16)
        for height in range(1, top_used + 1)
    ]
    scratch = [
        pltpu.VMEM((leaves + 2 * RIM + 1, num_vectors, points), BF16),
        pltpu.VMEM(leaf_basis.shape, BF16),
        pltpu.VMEM(near_blocks.shape, BF16),
        pltpu.VMEM(transfer_low.shape, BF16),
        pltpu.VMEM(coupling_low.shape, BF16),
        pltpu.VMEM(transfer_top.shape, BF16),
        pltpu.VMEM((top_used,) + coupling_top.shape[1:], BF16),
        pltpu.VMEM(vectors.shape, F32),
        pltpu.VMEM((coupling_low.shape[0], num_vectors, rank), F32),
        pltpu.VMEM((tree_devs + 1, num_vectors, 2 * rank), BF16),
        *boxes,
        pltpu.SemaphoreType.DMA((6 + top_used,)),
        pltpu.SemaphoreType.DMA((2 * low_levels,)),
        pltpu.SemaphoreType.DMA((2 * low_levels,)),
        pltpu.SemaphoreType.DMA,
        pltpu.SemaphoreType.DMA,
    ]
    sizes = (leaves, low_levels, tree_devs, num_sub, top_used, k_near, k_far)
    return pl.pallas_call(
        functools.partial(kernel, sizes),
        out_shape=jax.ShapeDtypeStruct(vectors.shape, BF16),
        in_specs=[pl.BlockSpec(memory_space=pltpu.SMEM)] * 4
        + [pl.BlockSpec(memory_space=pl.ANY)] * 7,
        out_specs=pl.BlockSpec(memory_space=pltpu.VMEM),
        scratch_shapes=scratch,
        compiler_params=pltpu.CompilerParams(
            collective_id=0, has_side_effects=True, vmem_limit_bytes=40 * 1024 * 1024
        ),
    )(
        near_list,
        near_mask,
        far_list,
        far_mask,
        vectors,
        leaf_basis,
        near_blocks,
        transfer_low,
        coupling_low,
        transfer_top,
        coupling_top,
    )


def solution(mesh):
    in_specs = (
        P(("copies", "leaf", "sub"), None, None),
        P(("copies", "leaf", "sub"), None, None),
        P(("copies", "leaf", "sub"), None, None, None),
        P(("leaf", "sub"), None),
        P(("leaf", "sub"), None),
        P(("copies", "leaf", "sub"), None, None),
        P(("copies", "leaf", "sub"), None, None, None),
        P(("leaf", "sub"), None),
        P(("leaf", "sub"), None),
        P("copies", None, None),
        P("copies", None, None, None),
    )
    out_specs = P(("copies", "leaf", "sub"), None, None)
    return jax.shard_map(
        per_device, mesh=mesh, in_specs=in_specs, out_specs=out_specs, check_vma=False
    )
```

```python
import functools

import jax
import jax.numpy as jnp
from jax import lax
from jax.experimental import pallas as pl
from jax.experimental.pallas import tpu as pltpu
from jax.sharding import PartitionSpec as P

RIM = 2
MESH = pl.DeviceIdType.MESH
F32 = jnp.float32
BF16 = jnp.bfloat16


def bdot(left, right, transposed=False):
    contract = 2 if transposed else 1
    return lax.dot_general(
        left, right, (((2,), (contract,)), ((0,), (0,))), preferred_element_type=F32
    )


def split(value):
    high = value.astype(BF16)
    low = (value - high.astype(F32)).astype(BF16)
    return high, low


def stacked(value):
    return jnp.concatenate(split(value), axis=-2)


def folded(value):
    half = value.shape[-2] // 2
    return value[..., :half, :] + value[..., half:, :]


def kernel(
    sizes,
    near_list_in,
    near_mask_in,
    far_list_in,
    far_mask_in,
    vectors,
    basis,
    near_blocks,
    transfer_low,
    coupling_low,
    transfer_top,
    coupling_top,
    out,
    near_list,
    near_mask,
    far_list,
    far_mask,
    vec_buf,
    basis_buf,
    near_buf,
    tlow_buf,
    clow_buf,
    ttop_buf,
    ctop_buf,
    near_acc,
    far_acc,
    roots,
    *rest,
):
    leaves, low_levels, tree_devs, num_sub, top_used, k_near, k_far = sizes
    level_bufs = rest[: low_levels - 1]
    top_bufs = rest[low_levels - 1 : low_levels - 1 + top_used]
    local_sem, rim_send, rim_recv, root_send, root_recv = rest[-5:]
    leaf_at = lax.axis_index("leaf")
    device = leaf_at * num_sub + lax.axis_index("sub")
    copy_at = lax.axis_index("copies")

    def place(index):
        return (copy_at, index // num_sub, index % num_sub)

    barrier = pltpu.get_barrier_semaphore()

    def greet(step, carry):
        pl.semaphore_signal(
            barrier, inc=1, device_id=place((device + step) % tree_devs), device_id_type=MESH
        )
        return carry

    lax.fori_loop(1, tree_devs, greet, 0, unroll=tree_devs <= 16)

    moves = [
        (vectors, vec_buf.at[pl.ds(RIM, leaves)]),
        (basis, basis_buf),
        (transfer_low, tlow_buf),
        (near_list_in, near_list),
        (near_mask_in, near_mask),
        (near_blocks, near_buf),
        (far_list_in, far_list),
        (far_mask_in, far_mask),
        (coupling_low, clow_buf),
        (transfer_top, ttop_buf),
    ]
    for height in range(1, top_used + 1):
        row = tree_devs - 2 * (tree_devs >> height) + device // (1 << height)
        moves.append((coupling_top.at[row], ctop_buf.at[height - 1]))
    copies = [
        pltpu.make_async_copy(source, target, local_sem.at[at])
        for at, (source, target) in enumerate(moves)
    ]
    for copy in copies:
        copy.start()

    starts = [2 * leaves - 2 * (leaves >> height) for height in range(low_levels)]
    counts = [leaves >> height for height in range(low_levels)]
    rims = [min(RIM, count) for count in counts]

    vec_buf[leaves + 2 * RIM] = jnp.zeros(vec_buf.shape[1:], BF16)
    for buf in level_bufs:
        buf[buf.shape[0] - 1] = jnp.zeros(buf.shape[1:], BF16)
    for buf in top_bufs:
        buf[buf.shape[0] - 1] = jnp.zeros(buf.shape[1:], BF16)
    roots[tree_devs] = jnp.zeros(roots.shape[1:], BF16)

    def rim_copies(buf, count, rim, at):
        to_right = pltpu.make_async_remote_copy(
            src_ref=buf.at[pl.ds(count, rim)],
            dst_ref=buf.at[pl.ds(0, rim)],
            send_sem=rim_send.at[2 * at],
            recv_sem=rim_recv.at[2 * at],
            device_id=place(device + 1),
            device_id_type=MESH,
        )
        to_left = pltpu.make_async_remote_copy(
            src_ref=buf.at[pl.ds(rim, rim)],
            dst_ref=buf.at[pl.ds(rim + count, rim)],
            send_sem=rim_send.at[2 * at + 1],
            recv_sem=rim_recv.at[2 * at + 1],
            device_id=place(device - 1),
            device_id_type=MESH,
        )
        return to_right, to_left

    rim_pairs = [rim_copies(vec_buf, leaves, RIM, low_levels - 1)]
    for height in range(low_levels - 1):
        rim_pairs.append(rim_copies(level_bufs[height], counts[height], rims[height], height))

    has_right = device < tree_devs - 1
    has_left = device > 0

    def send_rims(at):
        to_right, to_left = rim_pairs[at]

        @pl.when(has_right)
        def _():
            to_right.start()

        @pl.when(has_left)
        def _():
            to_left.start()

    def take_rims(at):
        to_right, to_left = rim_pairs[at]

        @pl.when(has_left)
        def _():
            to_right.wait_recv()

        @pl.when(has_right)
        def _():
            to_left.wait_recv()

    copies[0].wait()
    copies[1].wait()
    coefs = bdot(vec_buf[pl.ds(RIM, leaves)], basis_buf[...], transposed=True)
    pieces = stacked(coefs)
    level_bufs[0][pl.ds(rims[0], counts[0])] = pieces
    pl.semaphore_wait(barrier, tree_devs - 1)
    send_rims(0)
    send_rims(1)
    copies[2].wait()
    for height in range(1, low_levels):
        below = counts[height - 1]
        moved = folded(bdot(pieces, tlow_buf[pl.ds(starts[height - 1], below)]))
        moved = moved.reshape((below // 2, 2) + moved.shape[1:])
        coefs = moved[:, 0] + moved[:, 1]
        if height < low_levels - 1:
            pieces = stacked(coefs)
            level_bufs[height][pl.ds(rims[height], counts[height])] = pieces
            send_rims(height + 1)
    high, low = split(coefs[0])
    roots[device] = jnp.concatenate([high.astype(F32), low.astype(F32)], axis=-1).astype(BF16)

    def send_root(step, carry):
        pltpu.make_async_remote_copy(
            src_ref=roots.at[device],
            dst_ref=roots.at[device],
            send_sem=root_send,
            recv_sem=root_recv,
            device_id=place((device + step) % tree_devs),
            device_id_type=MESH,
        ).start()
        return carry

    lax.fori_loop(1, tree_devs, send_root, 0, unroll=tree_devs <= 16)

    take_rims(0)
    for copy in copies[3:6]:
        copy.wait()
    near_base = device * leaves - RIM

    def near_step(leaf, carry):
        sources = []
        for slot in range(k_near):
            spot = jnp.where(
                near_mask[slot, leaf] != 0,
                near_list[slot, leaf] - near_base,
                leaves + 2 * RIM,
            )
            sources.append(vec_buf[spot])
        blocks = near_buf[leaf]
        near_acc[leaf] = jnp.dot(
            jnp.concatenate(sources, axis=-1),
            blocks.reshape(blocks.shape[0] * blocks.shape[1], blocks.shape[2]),
            preferred_element_type=F32,
        )
        return carry

    lax.fori_loop(0, leaves, near_step, 0, unroll=True)

    for copy in copies[6:9]:
        copy.wait()
    for height in range(low_levels - 1):
        take_rims(height + 1)
        buf = level_bufs[height]
        far_base = device * counts[height] - rims[height]
        zero_spot = buf.shape[0] - 1

        def far_step(box, carry, buf=buf, far_base=far_base, zero_spot=zero_spot, height=height):
            row = starts[height] + box
            total = None
            for slot in range(k_far):
                spot = jnp.where(
                    far_mask[slot, row] != 0, far_list[slot, row] - far_base, zero_spot
                )
                term = jnp.dot(buf[spot], clow_buf[row, slot], preferred_element_type=F32)
                total = term if total is None else total + term
            far_acc[row] = folded(total)
            return carry

        lax.fori_loop(0, counts[height], far_step, 0, unroll=True)

    for copy in copies[9:]:
        copy.wait()
    arrived = roots.at[pl.ds(0, tree_devs - 1)]
    pltpu.make_async_copy(arrived, arrived, root_recv).wait()

    def doubled(matrix):
        return jnp.concatenate([matrix, matrix], axis=-2)

    pieces = roots[pl.ds(0, tree_devs)]
    for height in range(1, top_used + 1):
        below = tree_devs >> (height - 1)
        first = 2 * tree_devs - 2 * below
        mats = ttop_buf[pl.ds(first, below)]
        moved = bdot(pieces, doubled(mats)) if height == 1 else folded(bdot(pieces, mats))
        moved = moved.reshape((below // 2, 2) + moved.shape[1:])
        pieces = stacked(moved[:, 0] + moved[:, 1])
        top_bufs[height - 1][pl.ds(0, below // 2)] = pieces

    root_row = starts[low_levels - 1]
    downward = None
    for height in range(top_used, -1, -1):
        node = device // (1 << height)
        boxes = tree_devs >> height
        total = None
        if height == 0:
            for slot in range(k_far):
                spot = jnp.where(
                    far_mask[slot, root_row] != 0, far_list[slot, root_row], tree_devs
                )
                term = jnp.dot(
                    roots[spot], doubled(clow_buf[root_row, slot]), preferred_element_type=F32
                )
                total = term if total is None else total + term
        else:
            odd = node % 2
            for slot, (even_step, odd_step) in enumerate(((-2, -3), (2, -2), (3, 2))):
                source = node + jnp.where(odd == 1, odd_step, even_step)
                spot = jnp.where((source >= 0) & (source < boxes), source, boxes)
                term = jnp.dot(
                    top_bufs[height - 1][spot],
                    ctop_buf[height - 1, slot],
                    preferred_element_type=F32,
                )
                total = term if total is None else total + term
            total = folded(total)
        if downward is not None:
            matrix = ttop_buf[2 * tree_devs - 2 * boxes + node]
            total = total + folded(
                lax.dot_general(
                    stacked(downward), matrix, (((1,), (1,)), ((), ())), preferred_element_type=F32
                )
            )
        downward = total

    expanded = downward[None]
    for height in range(low_levels - 2, -1, -1):
        count = counts[height]
        spread = stacked(expanded)
        spread = jnp.broadcast_to(spread[:, None], (count // 2, 2) + spread.shape[1:])
        spread = spread.reshape((count,) + spread.shape[2:])
        mats = tlow_buf[pl.ds(starts[height], count)]
        expanded = far_acc[pl.ds(starts[height], count)] + folded(
            bdot(spread, mats, transposed=True)
        )
    leaf_term = folded(bdot(stacked(expanded), basis_buf[...]))
    out[...] = (near_acc[...] + leaf_term).astype(out.dtype)

    sent = roots.at[pl.ds(0, tree_devs - 1)]
    pltpu.make_async_copy(sent, sent, root_send).wait()
    for to_right, to_left in rim_pairs:

        @pl.when(has_right)
        def _(to_right=to_right):
            to_right.wait_send()

        @pl.when(has_left)
        def _(to_left=to_left):
            to_left.wait_send()


def per_device(
    vectors,
    leaf_basis,
    near_blocks,
    near_list,
    near_mask,
    transfer_low,
    coupling_low,
    far_list,
    far_mask,
    transfer_top,
    coupling_top,
):
    tree_devs = lax.axis_size(("leaf", "sub"))
    num_sub = lax.axis_size("sub")
    leaves, num_vectors, points = vectors.shape
    rank = leaf_basis.shape[1]
    k_near = near_blocks.shape[1]
    k_far = coupling_low.shape[1]
    low_levels = leaves.bit_length()
    top_used = max(tree_devs.bit_length() - 3, 0)
    counts = [leaves >> height for height in range(low_levels - 1)]
    boxes = [
        pltpu.VMEM((count + 2 * min(RIM, count) + 1, 2 * num_vectors, rank), BF16)
        for count in counts
    ] + [
        pltpu.VMEM(((tree_devs >> height) + 1, 2 * num_vectors, rank), BF16)
        for height in range(1, top_used + 1)
    ]
    scratch = [
        pltpu.SMEM(near_list.shape[::-1], jnp.int32),
        pltpu.SMEM(near_list.shape[::-1], jnp.int32),
        pltpu.SMEM(far_list.shape[::-1], jnp.int32),
        pltpu.SMEM(far_list.shape[::-1], jnp.int32),
        pltpu.VMEM((leaves + 2 * RIM + 1, num_vectors, points), BF16),
        pltpu.VMEM(leaf_basis.shape, BF16),
        pltpu.VMEM(near_blocks.shape, BF16),
        pltpu.VMEM(transfer_low.shape, BF16),
        pltpu.VMEM(coupling_low.shape, BF16),
        pltpu.VMEM(transfer_top.shape, BF16),
        pltpu.VMEM((top_used,) + coupling_top.shape[1:], BF16),
        pltpu.VMEM(vectors.shape, F32),
        pltpu.VMEM((coupling_low.shape[0], num_vectors, rank), F32),
        pltpu.VMEM((tree_devs + 1, num_vectors, 2 * rank), BF16),
        *boxes,
        pltpu.SemaphoreType.DMA((10 + top_used,)),
        pltpu.SemaphoreType.DMA((2 * low_levels,)),
        pltpu.SemaphoreType.DMA((2 * low_levels,)),
        pltpu.SemaphoreType.DMA,
        pltpu.SemaphoreType.DMA,
    ]
    sizes = (leaves, low_levels, tree_devs, num_sub, top_used, k_near, k_far)
    return pl.pallas_call(
        functools.partial(kernel, sizes),
        out_shape=jax.ShapeDtypeStruct(vectors.shape, BF16),
        in_specs=[pl.BlockSpec(memory_space=pltpu.HBM)] * 11,
        out_specs=pl.BlockSpec(memory_space=pltpu.VMEM),
        scratch_shapes=scratch,
        compiler_params=pltpu.CompilerParams(
            collective_id=0, has_side_effects=True, vmem_limit_bytes=60 * 1024 * 1024
        ),
    )(
        near_list.T,
        near_mask.T,
        far_list.T,
        far_mask.T,
        vectors,
        leaf_basis,
        near_blocks,
        transfer_low,
        coupling_low,
        transfer_top,
        coupling_top,
    )


def solution(mesh):
    in_specs = (
        P(("copies", "leaf", "sub"), None, None),
        P(("copies", "leaf", "sub"), None, None),
        P(("copies", "leaf", "sub"), None, None, None),
        P(("leaf", "sub"), None),
        P(("leaf", "sub"), None),
        P(("copies", "leaf", "sub"), None, None),
        P(("copies", "leaf", "sub"), None, None, None),
        P(("leaf", "sub"), None),
        P(("leaf", "sub"), None),
        P("copies", None, None),
        P("copies", None, None, None),
    )
    out_specs = P(("copies", "leaf", "sub"), None, None)
    return jax.shard_map(
        per_device, mesh=mesh, in_specs=in_specs, out_specs=out_specs, check_vma=False
    )
```

```python
import functools

import jax
import jax.numpy as jnp
from jax import lax
from jax.experimental import pallas as pl
from jax.experimental.pallas import tpu as pltpu
from jax.sharding import PartitionSpec as P

RIM = 2
MESH = pl.DeviceIdType.MESH
F32 = jnp.float32
BF16 = jnp.bfloat16


def bdot(left, right, transposed=False):
    contract = 2 if transposed else 1
    return lax.dot_general(
        left, right, (((2,), (contract,)), ((0,), (0,))), preferred_element_type=F32
    )


def split(value):
    high = value.astype(BF16)
    low = (value - high.astype(F32)).astype(BF16)
    return high, low


def stacked(value):
    return jnp.concatenate(split(value), axis=-2)


def folded(value):
    half = value.shape[-2] // 2
    return value[..., :half, :] + value[..., half:, :]


def kernel(
    sizes,
    near_list_in,
    near_mask_in,
    far_list_in,
    far_mask_in,
    vectors,
    basis,
    near_blocks,
    transfer_low,
    coupling_low,
    transfer_top,
    coupling_top,
    out,
    near_list,
    near_mask,
    far_list,
    far_mask,
    vec_buf,
    basis_buf,
    near_buf,
    tlow_buf,
    clow_buf,
    ttop_buf,
    ctop_buf,
    near_acc,
    far_acc,
    roots,
    *rest,
):
    leaves, low_levels, tree_devs, num_sub, top_used, k_near, k_far = sizes
    level_bufs = rest[: low_levels - 1]
    top_bufs = rest[low_levels - 1 : low_levels - 1 + top_used]
    local_sem, rim_send, rim_recv, root_send, root_recv = rest[-5:]
    leaf_at = lax.axis_index("leaf")
    device = leaf_at * num_sub + lax.axis_index("sub")
    copy_at = lax.axis_index("copies")

    def place(index):
        return (copy_at, index // num_sub, index % num_sub)

    barrier = pltpu.get_barrier_semaphore()

    def greet(step, carry):
        pl.semaphore_signal(
            barrier, inc=1, device_id=place((device + step) % tree_devs), device_id_type=MESH
        )
        return carry

    moves = [
        (vectors, vec_buf.at[pl.ds(RIM, leaves)]),
        (basis, basis_buf),
        (transfer_low, tlow_buf),
        (near_list_in, near_list),
        (near_mask_in, near_mask),
        (near_blocks, near_buf),
        (far_list_in, far_list),
        (far_mask_in, far_mask),
        (coupling_low, clow_buf),
        (transfer_top, ttop_buf),
    ]
    for height in range(1, top_used + 1):
        row = tree_devs - 2 * (tree_devs >> height) + device // (1 << height)
        moves.append((coupling_top.at[row], ctop_buf.at[height - 1]))
    copies = [
        pltpu.make_async_copy(source, target, local_sem.at[at])
        for at, (source, target) in enumerate(moves)
    ]
    for copy in copies[:3]:
        copy.start()
    lax.fori_loop(1, tree_devs, greet, 0, unroll=tree_devs <= 16)
    for copy in copies[3:]:
        copy.start()

    starts = [2 * leaves - 2 * (leaves >> height) for height in range(low_levels)]
    counts = [leaves >> height for height in range(low_levels)]
    rims = [min(RIM, count) for count in counts]

    vec_buf[leaves + 2 * RIM] = jnp.zeros(vec_buf.shape[1:], BF16)
    for buf in level_bufs:
        buf[buf.shape[0] - 1] = jnp.zeros(buf.shape[1:], BF16)
    for buf in top_bufs:
        buf[buf.shape[0] - 1] = jnp.zeros(buf.shape[1:], BF16)
    roots[tree_devs] = jnp.zeros(roots.shape[1:], BF16)

    def rim_copies(buf, count, rim, at):
        to_right = pltpu.make_async_remote_copy(
            src_ref=buf.at[pl.ds(count, rim)],
            dst_ref=buf.at[pl.ds(0, rim)],
            send_sem=rim_send.at[2 * at],
            recv_sem=rim_recv.at[2 * at],
            device_id=place(device + 1),
            device_id_type=MESH,
        )
        to_left = pltpu.make_async_remote_copy(
            src_ref=buf.at[pl.ds(rim, rim)],
            dst_ref=buf.at[pl.ds(rim + count, rim)],
            send_sem=rim_send.at[2 * at + 1],
            recv_sem=rim_recv.at[2 * at + 1],
            device_id=place(device - 1),
            device_id_type=MESH,
        )
        return to_right, to_left

    rim_pairs = [rim_copies(vec_buf, leaves, RIM, low_levels - 1)]
    for height in range(low_levels - 1):
        rim_pairs.append(rim_copies(level_bufs[height], counts[height], rims[height], height))

    has_right = device < tree_devs - 1
    has_left = device > 0

    def send_rims(at):
        to_right, to_left = rim_pairs[at]

        @pl.when(has_right)
        def _():
            to_right.start()

        @pl.when(has_left)
        def _():
            to_left.start()

    def take_rims(at):
        to_right, to_left = rim_pairs[at]

        @pl.when(has_left)
        def _():
            to_right.wait_recv()

        @pl.when(has_right)
        def _():
            to_left.wait_recv()

    copies[0].wait()
    copies[1].wait()
    coefs = bdot(vec_buf[pl.ds(RIM, leaves)], basis_buf[...], transposed=True)
    pieces = stacked(coefs)
    level_bufs[0][pl.ds(rims[0], counts[0])] = pieces
    copies[2].wait()
    for height in range(1, low_levels):
        below = counts[height - 1]
        moved = folded(bdot(pieces, tlow_buf[pl.ds(starts[height - 1], below)]))
        moved = moved.reshape((below // 2, 2) + moved.shape[1:])
        coefs = moved[:, 0] + moved[:, 1]
        if height < low_levels - 1:
            pieces = stacked(coefs)
            level_bufs[height][pl.ds(rims[height], counts[height])] = pieces
    high, low = split(coefs[0])
    roots[device] = jnp.concatenate([high.astype(F32), low.astype(F32)], axis=-1).astype(BF16)

    pl.semaphore_wait(barrier, tree_devs - 1)

    def send_root(step, carry):
        pltpu.make_async_remote_copy(
            src_ref=roots.at[device],
            dst_ref=roots.at[device],
            send_sem=root_send,
            recv_sem=root_recv,
            device_id=place((device + step) % tree_devs),
            device_id_type=MESH,
        ).start()
        return carry

    lax.fori_loop(1, tree_devs, send_root, 0, unroll=tree_devs <= 16)
    for at in range(low_levels):
        send_rims(at)

    take_rims(0)
    for copy in copies[3:6]:
        copy.wait()
    near_base = device * leaves - RIM

    def near_step(leaf, carry):
        sources = []
        for slot in range(k_near):
            spot = jnp.where(
                near_mask[slot, leaf] != 0,
                near_list[slot, leaf] - near_base,
                leaves + 2 * RIM,
            )
            sources.append(vec_buf[spot])
        blocks = near_buf[leaf]
        near_acc[leaf] = jnp.dot(
            jnp.concatenate(sources, axis=-1),
            blocks.reshape(blocks.shape[0] * blocks.shape[1], blocks.shape[2]),
            preferred_element_type=F32,
        )
        return carry

    lax.fori_loop(0, leaves, near_step, 0, unroll=True)

    for copy in copies[6:9]:
        copy.wait()
    for height in range(low_levels - 1):
        take_rims(height + 1)
        buf = level_bufs[height]
        far_base = device * counts[height] - rims[height]
        zero_spot = buf.shape[0] - 1

        def far_step(box, carry, buf=buf, far_base=far_base, zero_spot=zero_spot, height=height):
            row = starts[height] + box
            total = None
            for slot in range(k_far):
                spot = jnp.where(
                    far_mask[slot, row] != 0, far_list[slot, row] - far_base, zero_spot
                )
                term = jnp.dot(buf[spot], clow_buf[row, slot], preferred_element_type=F32)
                total = term if total is None else total + term
            far_acc[row] = folded(total)
            return carry

        lax.fori_loop(0, counts[height], far_step, 0, unroll=True)

    for copy in copies[9:]:
        copy.wait()
    arrived = roots.at[pl.ds(0, tree_devs - 1)]
    pltpu.make_async_copy(arrived, arrived, root_recv).wait()

    def doubled(matrix):
        return jnp.concatenate([matrix, matrix], axis=-2)

    pieces = roots[pl.ds(0, tree_devs)]
    for height in range(1, top_used + 1):
        below = tree_devs >> (height - 1)
        first = 2 * tree_devs - 2 * below
        mats = ttop_buf[pl.ds(first, below)]
        moved = bdot(pieces, doubled(mats)) if height == 1 else folded(bdot(pieces, mats))
        moved = moved.reshape((below // 2, 2) + moved.shape[1:])
        pieces = stacked(moved[:, 0] + moved[:, 1])
        top_bufs[height - 1][pl.ds(0, below // 2)] = pieces

    root_row = starts[low_levels - 1]
    downward = None
    for height in range(top_used, -1, -1):
        node = device // (1 << height)
        boxes = tree_devs >> height
        total = None
        if height == 0:
            for slot in range(k_far):
                spot = jnp.where(
                    far_mask[slot, root_row] != 0, far_list[slot, root_row], tree_devs
                )
                term = jnp.dot(
                    roots[spot], doubled(clow_buf[root_row, slot]), preferred_element_type=F32
                )
                total = term if total is None else total + term
        else:
            odd = node % 2
            for slot, (even_step, odd_step) in enumerate(((-2, -3), (2, -2), (3, 2))):
                source = node + jnp.where(odd == 1, odd_step, even_step)
                spot = jnp.where((source >= 0) & (source < boxes), source, boxes)
                term = jnp.dot(
                    top_bufs[height - 1][spot],
                    ctop_buf[height - 1, slot],
                    preferred_element_type=F32,
                )
                total = term if total is None else total + term
            total = folded(total)
        if downward is not None:
            matrix = ttop_buf[2 * tree_devs - 2 * boxes + node]
            total = total + folded(
                lax.dot_general(
                    stacked(downward), matrix, (((1,), (1,)), ((), ())), preferred_element_type=F32
                )
            )
        downward = total

    expanded = downward[None]
    for height in range(low_levels - 2, -1, -1):
        count = counts[height]
        spread = stacked(expanded)
        spread = jnp.broadcast_to(spread[:, None], (count // 2, 2) + spread.shape[1:])
        spread = spread.reshape((count,) + spread.shape[2:])
        mats = tlow_buf[pl.ds(starts[height], count)]
        expanded = far_acc[pl.ds(starts[height], count)] + folded(
            bdot(spread, mats, transposed=True)
        )
    leaf_term = folded(bdot(stacked(expanded), basis_buf[...]))
    out[...] = (near_acc[...] + leaf_term).astype(out.dtype)

    sent = roots.at[pl.ds(0, tree_devs - 1)]
    pltpu.make_async_copy(sent, sent, root_send).wait()
    for to_right, to_left in rim_pairs:

        @pl.when(has_right)
        def _(to_right=to_right):
            to_right.wait_send()

        @pl.when(has_left)
        def _(to_left=to_left):
            to_left.wait_send()


def per_device(
    vectors,
    leaf_basis,
    near_blocks,
    near_list,
    near_mask,
    transfer_low,
    coupling_low,
    far_list,
    far_mask,
    transfer_top,
    coupling_top,
):
    tree_devs = lax.axis_size(("leaf", "sub"))
    num_sub = lax.axis_size("sub")
    leaves, num_vectors, points = vectors.shape
    rank = leaf_basis.shape[1]
    k_near = near_blocks.shape[1]
    k_far = coupling_low.shape[1]
    low_levels = leaves.bit_length()
    top_used = max(tree_devs.bit_length() - 3, 0)
    counts = [leaves >> height for height in range(low_levels - 1)]
    boxes = [
        pltpu.VMEM((count + 2 * min(RIM, count) + 1, 2 * num_vectors, rank), BF16)
        for count in counts
    ] + [
        pltpu.VMEM(((tree_devs >> height) + 1, 2 * num_vectors, rank), BF16)
        for height in range(1, top_used + 1)
    ]
    scratch = [
        pltpu.SMEM(near_list.shape[::-1], jnp.int32),
        pltpu.SMEM(near_list.shape[::-1], jnp.int32),
        pltpu.SMEM(far_list.shape[::-1], jnp.int32),
        pltpu.SMEM(far_list.shape[::-1], jnp.int32),
        pltpu.VMEM((leaves + 2 * RIM + 1, num_vectors, points), BF16),
        pltpu.VMEM(leaf_basis.shape, BF16),
        pltpu.VMEM(near_blocks.shape, BF16),
        pltpu.VMEM(transfer_low.shape, BF16),
        pltpu.VMEM(coupling_low.shape, BF16),
        pltpu.VMEM(transfer_top.shape, BF16),
        pltpu.VMEM((top_used,) + coupling_top.shape[1:], BF16),
        pltpu.VMEM(vectors.shape, F32),
        pltpu.VMEM((coupling_low.shape[0], num_vectors, rank), F32),
        pltpu.VMEM((tree_devs + 1, num_vectors, 2 * rank), BF16),
        *boxes,
        pltpu.SemaphoreType.DMA((10 + top_used,)),
        pltpu.SemaphoreType.DMA((2 * low_levels,)),
        pltpu.SemaphoreType.DMA((2 * low_levels,)),
        pltpu.SemaphoreType.DMA,
        pltpu.SemaphoreType.DMA,
    ]
    sizes = (leaves, low_levels, tree_devs, num_sub, top_used, k_near, k_far)
    return pl.pallas_call(
        functools.partial(kernel, sizes),
        out_shape=pltpu.VMEM(vectors.shape, BF16),
        in_specs=[pl.BlockSpec(memory_space=pltpu.HBM)] * 11,
        out_specs=pl.BlockSpec(memory_space=pltpu.VMEM),
        scratch_shapes=scratch,
        compiler_params=pltpu.CompilerParams(
            collective_id=0, has_side_effects=True, vmem_limit_bytes=60 * 1024 * 1024
        ),
    )(
        near_list.T,
        near_mask.T,
        far_list.T,
        far_mask.T,
        vectors,
        leaf_basis,
        near_blocks,
        transfer_low,
        coupling_low,
        transfer_top,
        coupling_top,
    )


def solution(mesh):
    in_specs = (
        P(("copies", "leaf", "sub"), None, None),
        P(("copies", "leaf", "sub"), None, None),
        P(("copies", "leaf", "sub"), None, None, None),
        P(("leaf", "sub"), None),
        P(("leaf", "sub"), None),
        P(("copies", "leaf", "sub"), None, None),
        P(("copies", "leaf", "sub"), None, None, None),
        P(("leaf", "sub"), None),
        P(("leaf", "sub"), None),
        P("copies", None, None),
        P("copies", None, None, None),
    )
    out_specs = P(("copies", "leaf", "sub"), None, None)
    return jax.shard_map(
        per_device, mesh=mesh, in_specs=in_specs, out_specs=out_specs, check_vma=False
    )
```

```python
import functools

import jax
import jax.numpy as jnp
from jax import lax
from jax.experimental import pallas as pl
from jax.experimental.pallas import tpu as pltpu
from jax.sharding import PartitionSpec as P

RIM = 2
MESH = pl.DeviceIdType.MESH
F32 = jnp.float32
BF16 = jnp.bfloat16


def bdot(left, right, transposed=False):
    contract = 2 if transposed else 1
    return lax.dot_general(
        left, right, (((2,), (contract,)), ((0,), (0,))), preferred_element_type=F32
    )


def split(value):
    high = value.astype(BF16)
    low = (value - high.astype(F32)).astype(BF16)
    return high, low


def stacked(value):
    return jnp.concatenate(split(value), axis=-2)


def folded(value):
    half = value.shape[-2] // 2
    return value[..., :half, :] + value[..., half:, :]


def packed(value):
    high = value.astype(BF16).astype(F32)
    return jnp.concatenate([high, value - high], axis=-1).astype(BF16)


def doubled(matrix):
    return jnp.concatenate([matrix, matrix], axis=-2)


def dot(left, right, transposed=False):
    contract = 1 if transposed else 0
    return lax.dot_general(
        left, right, (((1,), (contract,)), ((), ())), preferred_element_type=F32
    )


def kernel(
    sizes,
    near_list_in,
    near_mask_in,
    far_list_in,
    far_mask_in,
    vectors,
    basis,
    near_blocks,
    transfer_low,
    coupling_low,
    transfer_top,
    coupling_top,
    out,
    near_list,
    near_mask,
    far_list,
    far_mask,
    vec_buf,
    basis_buf,
    near_buf,
    tlow_buf,
    clow_buf,
    ttop_buf,
    ctop_buf,
    near_acc,
    far_acc,
    roots,
    *rest,
):
    leaves, low_levels, tree_devs, num_sub, top_used, k_near, k_far = sizes
    level_bufs = rest[: low_levels - 1]
    rim_out, rim_in, path_buf, leaf_ways = rest[low_levels - 1 : -5]
    local_sem, rim_send, rim_recv, root_send, root_recv = rest[-5:]
    leaf_at = lax.axis_index("leaf")
    device = leaf_at * num_sub + lax.axis_index("sub")
    copy_at = lax.axis_index("copies")

    def place(index):
        return (copy_at, index // num_sub, index % num_sub)

    barrier = pltpu.get_barrier_semaphore()

    def greet(step, carry):
        pl.semaphore_signal(
            barrier, inc=1, device_id=place((device + step) % tree_devs), device_id_type=MESH
        )
        return carry

    moves = [
        (vectors, vec_buf.at[pl.ds(RIM, leaves)]),
        (basis, basis_buf),
        (transfer_low, tlow_buf),
        (near_list_in, near_list),
        (near_mask_in, near_mask),
        (near_blocks, near_buf),
        (far_list_in, far_list),
        (far_mask_in, far_mask),
        (coupling_low, clow_buf),
        (transfer_top, ttop_buf),
    ]
    for height in range(1, top_used + 1):
        row = tree_devs - 2 * (tree_devs >> height) + device // (1 << height)
        moves.append((coupling_top.at[row], ctop_buf.at[height - 1]))
    copies = [
        pltpu.make_async_copy(source, target, local_sem.at[at])
        for at, (source, target) in enumerate(moves)
    ]
    for copy in copies[:3]:
        copy.start()
    lax.fori_loop(1, tree_devs, greet, 0, unroll=tree_devs <= 16)
    for copy in copies[3:]:
        copy.start()

    starts = [2 * leaves - 2 * (leaves >> height) for height in range(low_levels)]
    counts = [leaves >> height for height in range(low_levels)]
    rims = [min(RIM, count) for count in counts]

    vec_buf[leaves + 2 * RIM] = jnp.zeros(vec_buf.shape[1:], BF16)
    for buf in level_bufs:
        buf[buf.shape[0] - 1] = jnp.zeros(buf.shape[1:], BF16)
    roots[tree_devs] = jnp.zeros(roots.shape[1:], BF16)

    parts = [(vec_buf, leaves, RIM)]
    parts += [(level_bufs[height], counts[height], rims[height]) for height in range(low_levels - 1)]

    to_right, to_left = [
        pltpu.make_async_remote_copy(
            src_ref=rim_out.at[side],
            dst_ref=rim_in.at[side],
            send_sem=rim_send.at[side],
            recv_sem=rim_recv.at[side],
            device_id=place(device + step),
            device_id_type=MESH,
        )
        for side, step in ((0, 1), (1, -1))
    ]
    has_right = device < tree_devs - 1
    has_left = device > 0

    copies[0].wait()
    copies[1].wait()
    coefs = bdot(vec_buf[pl.ds(RIM, leaves)], basis_buf[...], transposed=True)
    level_coefs = [coefs]
    copies[2].wait()
    for height in range(1, low_levels):
        below = counts[height - 1]
        moved = folded(bdot(stacked(coefs), tlow_buf[pl.ds(starts[height - 1], below)]))
        moved = moved.reshape((below // 2, 2) + moved.shape[1:])
        coefs = moved[:, 0] + moved[:, 1]
        level_coefs.append(coefs)
    roots[device] = packed(coefs[0])
    pl.semaphore_wait(barrier, tree_devs - 1)

    def send_root(step, carry):
        pltpu.make_async_remote_copy(
            src_ref=roots.at[device],
            dst_ref=roots.at[device],
            send_sem=root_send,
            recv_sem=root_recv,
            device_id=place((device + step) % tree_devs),
            device_id_type=MESH,
        ).start()
        return carry

    lax.fori_loop(1, tree_devs, send_root, 0, unroll=tree_devs <= 16)

    for height in range(low_levels - 1):
        level_bufs[height][pl.ds(rims[height], counts[height])] = packed(level_coefs[height])
    at = 0
    for buf, count, rim in parts:
        rim_out[0, pl.ds(at, rim)] = buf[pl.ds(count, rim)]
        rim_out[1, pl.ds(at, rim)] = buf[pl.ds(rim, rim)]
        at += rim

    @pl.when(has_right)
    def _():
        to_right.start()

    @pl.when(has_left)
    def _():
        to_left.start()

    for copy in copies[3:]:
        copy.wait()

    def first_of(height):
        return 2 * tree_devs - 2 * (tree_devs >> height)

    sources = []
    root_row = starts[low_levels - 1]
    for slot in range(k_far):
        spot = jnp.where(far_mask[slot, root_row] != 0, far_list[slot, root_row], tree_devs)
        path_buf[len(sources)] = packed(clow_buf[root_row, slot].astype(F32))
        sources.append(spot)

    def expand(height, box, inside, matrix):
        if height == 0:
            path_buf[len(sources)] = packed(matrix)
            sources.append(jnp.where(inside, box, tree_devs))
            return
        mats = ttop_buf[pl.ds(first_of(height - 1) + 2 * box, 2)]
        mats = mats.reshape(2 * mats.shape[1], mats.shape[2])
        high, low = split(matrix)
        both = dot(mats, high) + dot(mats, low)
        rank = matrix.shape[0]
        expand(height - 1, 2 * box, inside, both[:rank])
        expand(height - 1, 2 * box + 1, inside, both[rank:])

    for height in range(1, top_used + 1):
        node = device // (1 << height)
        boxes = tree_devs >> height
        chain = ctop_buf[height - 1]
        rank = chain.shape[1]
        chain = chain.reshape(chain.shape[0] * rank, chain.shape[2])
        for step in range(height - 1, -1, -1):
            matrix = ttop_buf[first_of(step) + device // (1 << step)]
            if step == height - 1:
                chain = dot(chain, matrix, transposed=True)
            else:
                chain = folded(dot(stacked(chain), matrix, transposed=True))
        odd = node % 2
        for slot, (even_step, odd_step) in enumerate(((-2, -3), (2, -2), (3, 2))):
            box = node + jnp.where(odd == 1, odd_step, even_step)
            inside = (box >= 0) & (box < boxes)
            box = jnp.where(inside, box, 0)
            expand(height, box, inside, chain[slot * rank : (slot + 1) * rank])

    rank = tlow_buf.shape[1]
    rows = lax.broadcasted_iota(jnp.int32, (rank, rank), 0)
    columns = lax.broadcasted_iota(jnp.int32, (rank, rank), 1)
    unit = jnp.where(rows == columns, 1.0, 0.0).astype(BF16)
    ways = [unit]
    for height in range(low_levels - 2, -1, -1):
        following = []
        for box in range(counts[height]):
            way = ways[box // 2]
            moved = dot(way, tlow_buf[starts[height] + box], transposed=True)
            if height == low_levels - 2:
                moved = moved.astype(BF16)
            else:
                moved = stacked(moved if way.shape[0] == rank else folded(moved))
            following.append(moved)
        ways = following
    for leaf in range(leaves):
        moved = dot(ways[leaf], basis_buf[leaf])
        leaf_ways[leaf] = stacked(moved if ways[leaf].shape[0] == rank else folded(moved))

    @pl.when(has_left)
    def _():
        to_right.wait_recv()

    @pl.when(has_right)
    def _():
        to_left.wait_recv()

    at = 0
    for buf, count, rim in parts:
        buf[pl.ds(0, rim)] = rim_in[0, pl.ds(at, rim)]
        buf[pl.ds(rim + count, rim)] = rim_in[1, pl.ds(at, rim)]
        at += rim

    near_base = device * leaves - RIM

    def near_step(leaf, carry):
        beside = []
        for slot in range(k_near):
            spot = jnp.where(
                near_mask[slot, leaf] != 0,
                near_list[slot, leaf] - near_base,
                leaves + 2 * RIM,
            )
            beside.append(vec_buf[spot])
        blocks = near_buf[leaf]
        near_acc[leaf] = dot(
            jnp.concatenate(beside, axis=-1),
            blocks.reshape(blocks.shape[0] * blocks.shape[1], blocks.shape[2]),
        )
        return carry

    lax.fori_loop(0, leaves, near_step, 0, unroll=True)

    for height in range(low_levels - 1):
        buf = level_bufs[height]
        far_base = device * counts[height] - rims[height]
        zero_spot = buf.shape[0] - 1

        def far_step(box, carry, buf=buf, far_base=far_base, zero_spot=zero_spot, height=height):
            row = starts[height] + box
            total = None
            for slot in range(k_far):
                spot = jnp.where(
                    far_mask[slot, row] != 0, far_list[slot, row] - far_base, zero_spot
                )
                term = dot(buf[spot], doubled(clow_buf[row, slot]))
                total = term if total is None else total + term
            far_acc[row] = total
            return carry

        lax.fori_loop(0, counts[height], far_step, 0, unroll=True)

    expanded = None
    for height in range(low_levels - 2, -1, -1):
        count = counts[height]
        own = far_acc[pl.ds(starts[height], count)]
        if expanded is not None:
            spread = stacked(expanded)
            spread = jnp.broadcast_to(spread[:, None], (count // 2, 2) + spread.shape[1:])
            spread = spread.reshape((count,) + spread.shape[2:])
            mats = tlow_buf[pl.ds(starts[height], count)]
            own = own + folded(bdot(spread, mats, transposed=True))
        expanded = own
    near_acc[...] = near_acc[...] + folded(bdot(stacked(expanded), basis_buf[...]))

    arrived = roots.at[pl.ds(0, tree_devs - 1)]
    pltpu.make_async_copy(arrived, arrived, root_recv).wait()
    total = None
    for at, spot in enumerate(sources):
        term = dot(roots[spot], doubled(path_buf[at]))
        total = term if total is None else total + term
    downward = stacked(total + pltpu.roll(total, rank, 1))
    for leaf in range(leaves):
        out[leaf] = (near_acc[leaf] + folded(dot(downward, leaf_ways[leaf]))).astype(out.dtype)

    sent = roots.at[pl.ds(0, tree_devs - 1)]
    pltpu.make_async_copy(sent, sent, root_send).wait()

    @pl.when(has_right)
    def _():
        to_right.wait_send()

    @pl.when(has_left)
    def _():
        to_left.wait_send()


def per_device(
    vectors,
    leaf_basis,
    near_blocks,
    near_list,
    near_mask,
    transfer_low,
    coupling_low,
    far_list,
    far_mask,
    transfer_top,
    coupling_top,
):
    tree_devs = lax.axis_size(("leaf", "sub"))
    num_sub = lax.axis_size("sub")
    leaves, num_vectors, points = vectors.shape
    rank = leaf_basis.shape[1]
    k_near = near_blocks.shape[1]
    k_far = coupling_low.shape[1]
    low_levels = leaves.bit_length()
    top_used = max(tree_devs.bit_length() - 3, 0)
    counts = [leaves >> height for height in range(low_levels - 1)]
    boxes = [
        pltpu.VMEM((count + 2 * min(RIM, count) + 1, num_vectors, 2 * rank), BF16)
        for count in counts
    ]
    rim_boxes = RIM + sum(min(RIM, count) for count in counts)
    paths = k_far * sum(1 << height for height in range(top_used + 1))
    scratch = [
        pltpu.SMEM(near_list.shape[::-1], jnp.int32),
        pltpu.SMEM(near_list.shape[::-1], jnp.int32),
        pltpu.SMEM(far_list.shape[::-1], jnp.int32),
        pltpu.SMEM(far_list.shape[::-1], jnp.int32),
        pltpu.VMEM((leaves + 2 * RIM + 1, num_vectors, points), BF16),
        pltpu.VMEM(leaf_basis.shape, BF16),
        pltpu.VMEM(near_blocks.shape, BF16),
        pltpu.VMEM(transfer_low.shape, BF16),
        pltpu.VMEM(coupling_low.shape, BF16),
        pltpu.VMEM(transfer_top.shape, BF16),
        pltpu.VMEM((top_used,) + coupling_top.shape[1:], BF16),
        pltpu.VMEM(vectors.shape, F32),
        pltpu.VMEM((coupling_low.shape[0], num_vectors, rank), F32),
        pltpu.VMEM((tree_devs + 1, num_vectors, 2 * rank), BF16),
        *boxes,
        pltpu.VMEM((2, rim_boxes, num_vectors, points), BF16),
        pltpu.VMEM((2, rim_boxes, num_vectors, points), BF16),
        pltpu.VMEM((paths, rank, 2 * rank), BF16),
        pltpu.VMEM((leaves, 2 * rank, points), BF16),
        pltpu.SemaphoreType.DMA((10 + top_used,)),
        pltpu.SemaphoreType.DMA((2,)),
        pltpu.SemaphoreType.DMA((2,)),
        pltpu.SemaphoreType.DMA,
        pltpu.SemaphoreType.DMA,
    ]
    sizes = (leaves, low_levels, tree_devs, num_sub, top_used, k_near, k_far)
    return pl.pallas_call(
        functools.partial(kernel, sizes),
        out_shape=pltpu.VMEM(vectors.shape, BF16),
        in_specs=[pl.BlockSpec(memory_space=pltpu.HBM)] * 11,
        out_specs=pl.BlockSpec(memory_space=pltpu.VMEM),
        scratch_shapes=scratch,
        compiler_params=pltpu.CompilerParams(
            collective_id=0, has_side_effects=True, vmem_limit_bytes=60 * 1024 * 1024
        ),
    )(
        near_list.T,
        near_mask.T,
        far_list.T,
        far_mask.T,
        vectors,
        leaf_basis,
        near_blocks,
        transfer_low,
        coupling_low,
        transfer_top,
        coupling_top,
    )


def solution(mesh):
    in_specs = (
        P(("copies", "leaf", "sub"), None, None),
        P(("copies", "leaf", "sub"), None, None),
        P(("copies", "leaf", "sub"), None, None, None),
        P(("leaf", "sub"), None),
        P(("leaf", "sub"), None),
        P(("copies", "leaf", "sub"), None, None),
        P(("copies", "leaf", "sub"), None, None, None),
        P(("leaf", "sub"), None),
        P(("leaf", "sub"), None),
        P("copies", None, None),
        P("copies", None, None, None),
    )
    out_specs = P(("copies", "leaf", "sub"), None, None)
    return jax.shard_map(
        per_device, mesh=mesh, in_specs=in_specs, out_specs=out_specs, check_vma=False
    )
```

```python
import functools

import jax
import jax.numpy as jnp
from jax import lax
from jax.experimental import pallas as pl
from jax.experimental.pallas import tpu as pltpu
from jax.sharding import PartitionSpec as P

RIM = 2
MESH = pl.DeviceIdType.MESH
F32 = jnp.float32
BF16 = jnp.bfloat16


def bdot(left, right, transposed=False):
    contract = 2 if transposed else 1
    return lax.dot_general(
        left, right, (((2,), (contract,)), ((0,), (0,))), preferred_element_type=F32
    )


def split(value):
    high = value.astype(BF16)
    low = (value - high.astype(F32)).astype(BF16)
    return high, low


def stacked(value):
    return jnp.concatenate(split(value), axis=-2)


def folded(value):
    half = value.shape[-2] // 2
    return value[..., :half, :] + value[..., half:, :]


def packed(value):
    high = value.astype(BF16).astype(F32)
    return jnp.concatenate([high, value - high], axis=-1).astype(BF16)


def packed_twin(value):
    high = value.astype(BF16).astype(F32)
    lanes = lax.broadcasted_iota(jnp.int32, value.shape, value.ndim - 1)
    return jnp.where(lanes < value.shape[-1] // 2, high, value - high).astype(BF16)


def unpacked(pair):
    rank = pair.shape[-1] // 2
    return jnp.concatenate([pair[..., :rank], pair[..., rank:]], axis=-2)


def twin(value):
    return value + pltpu.roll(value, value.shape[-1] // 2, value.ndim - 1)


def doubled(matrix):
    return jnp.concatenate([matrix, matrix], axis=-2)


def dot(left, right, transposed=False):
    contract = 1 if transposed else 0
    return lax.dot_general(
        left, right, (((1,), (contract,)), ((), ())), preferred_element_type=F32
    )


def kernel(
    sizes,
    near_list_in,
    near_mask_in,
    far_list_in,
    far_mask_in,
    vectors,
    basis,
    near_blocks,
    transfer_low,
    coupling_low,
    transfer_top,
    coupling_top,
    out,
    near_list,
    near_mask,
    far_list,
    far_mask,
    vec_buf,
    basis_buf,
    near_buf,
    tlow_buf,
    clow_buf,
    ttop_buf,
    ctop_buf,
    near_acc,
    far_acc,
    roots,
    *rest,
):
    leaves, low_levels, tree_devs, num_sub, top_used, k_near, k_far = sizes
    level_bufs = rest[: low_levels - 1]
    rim_out, rim_in, path_buf, leaf_ways = rest[low_levels - 1 : -5]
    local_sem, rim_send, rim_recv, root_send, root_recv = rest[-5:]
    leaf_at = lax.axis_index("leaf")
    device = leaf_at * num_sub + lax.axis_index("sub")
    copy_at = lax.axis_index("copies")

    def place(index):
        return (copy_at, index // num_sub, index % num_sub)

    barrier = pltpu.get_barrier_semaphore()

    def greet(step, carry):
        pl.semaphore_signal(
            barrier, inc=1, device_id=place((device + step) % tree_devs), device_id_type=MESH
        )
        return carry

    moves = [
        (vectors, vec_buf.at[pl.ds(RIM, leaves)]),
        (basis, basis_buf),
        (transfer_low, tlow_buf),
        (near_list_in, near_list),
        (near_mask_in, near_mask),
        (near_blocks, near_buf),
        (far_list_in, far_list),
        (far_mask_in, far_mask),
        (coupling_low, clow_buf),
        (transfer_top, ttop_buf),
    ]
    for height in range(1, top_used + 1):
        row = tree_devs - 2 * (tree_devs >> height) + device // (1 << height)
        moves.append((coupling_top.at[row], ctop_buf.at[height - 1]))
    copies = [
        pltpu.make_async_copy(source, target, local_sem.at[at])
        for at, (source, target) in enumerate(moves)
    ]
    for copy in copies[:3]:
        copy.start()
    lax.fori_loop(1, tree_devs, greet, 0, unroll=tree_devs <= 16)
    for copy in copies[3:]:
        copy.start()

    starts = [2 * leaves - 2 * (leaves >> height) for height in range(low_levels)]
    counts = [leaves >> height for height in range(low_levels)]
    rims = [min(RIM, count) for count in counts]

    vec_buf[leaves + 2 * RIM] = jnp.zeros(vec_buf.shape[1:], BF16)
    for buf in level_bufs:
        buf[buf.shape[0] - 1] = jnp.zeros(buf.shape[1:], BF16)
    roots[tree_devs] = jnp.zeros(roots.shape[1:], BF16)

    to_right, to_left = [
        pltpu.make_async_remote_copy(
            src_ref=rim_out.at[side],
            dst_ref=rim_in.at[side],
            send_sem=rim_send.at[side],
            recv_sem=rim_recv.at[side],
            device_id=place(device + step),
            device_id_type=MESH,
        )
        for side, step in ((0, 1), (1, -1))
    ]
    has_right = device < tree_devs - 1
    has_left = device > 0

    copies[0].wait()
    copies[1].wait()
    coefs = bdot(vec_buf[pl.ds(RIM, leaves)], basis_buf[...], transposed=True)
    level_coefs = [coefs]
    pieces = []
    copies[2].wait()
    for height in range(1, low_levels):
        below = counts[height - 1]
        pieces.append(stacked(coefs))
        moved = folded(bdot(pieces[-1], tlow_buf[pl.ds(starts[height - 1], below)]))
        moved = moved.reshape((below // 2, 2) + moved.shape[1:])
        coefs = moved[:, 0] + moved[:, 1]
        level_coefs.append(coefs)
    roots[device] = packed(coefs[0])
    pl.semaphore_wait(barrier, tree_devs - 1)

    def send_root(step, carry):
        pltpu.make_async_remote_copy(
            src_ref=roots.at[device],
            dst_ref=roots.at[device],
            send_sem=root_send,
            recv_sem=root_recv,
            device_id=place((device + step) % tree_devs),
            device_id_type=MESH,
        ).start()
        return carry

    lax.fori_loop(1, tree_devs, send_root, 0, unroll=tree_devs <= 16)

    rim_out[0, pl.ds(0, RIM)] = vec_buf[pl.ds(leaves, RIM)]
    rim_out[1, pl.ds(0, RIM)] = vec_buf[pl.ds(RIM, RIM)]
    at = RIM
    for count, rim, coefs in zip(counts, rims, level_coefs[:-1]):
        rim_out[0, pl.ds(at, rim)] = packed(coefs[count - rim :])
        rim_out[1, pl.ds(at, rim)] = packed(coefs[:rim])
        at += rim

    @pl.when(has_right)
    def _():
        to_right.start()

    @pl.when(has_left)
    def _():
        to_left.start()

    for height in range(low_levels - 1):
        level_bufs[height][pl.ds(rims[height], counts[height])] = pieces[height]
    for copy in copies[3:]:
        copy.wait()

    def first_of(height):
        return 2 * tree_devs - 2 * (tree_devs >> height)

    sources = []
    root_row = starts[low_levels - 1]
    for slot in range(k_far):
        spot = jnp.where(far_mask[slot, root_row] != 0, far_list[slot, root_row], tree_devs)
        near_path = clow_buf[root_row, slot]
        path_buf[len(sources)] = jnp.concatenate([near_path, jnp.zeros_like(near_path)], axis=-1)
        sources.append(spot)

    def expand(height, box, inside, matrix):
        matrix = packed_twin(matrix)
        if height == 0:
            path_buf[len(sources)] = matrix
            sources.append(jnp.where(inside, box, tree_devs))
            return
        mats = ttop_buf[pl.ds(first_of(height - 1) + 2 * box, 2)]
        mats = mats.reshape(2 * mats.shape[1], mats.shape[2])
        both = twin(dot(mats, matrix))
        rank = matrix.shape[0]
        expand(height - 1, 2 * box, inside, both[:rank])
        expand(height - 1, 2 * box + 1, inside, both[rank:])

    for height in range(1, top_used + 1):
        node = device // (1 << height)
        boxes = tree_devs >> height
        chain = ctop_buf[height - 1]
        rank = chain.shape[1]
        chain = chain.reshape(chain.shape[0] * rank, chain.shape[2])
        for step in range(height - 1, -1, -1):
            matrix = ttop_buf[first_of(step) + device // (1 << step)]
            if step == 0:
                matrix = doubled(matrix)
            if step == height - 1:
                chain = dot(chain, matrix, transposed=True)
            else:
                chain = folded(dot(stacked(chain), matrix, transposed=True))
        odd = node % 2
        for slot, (even_step, odd_step) in enumerate(((-2, -3), (2, -2), (3, 2))):
            box = node + jnp.where(odd == 1, odd_step, even_step)
            inside = (box >= 0) & (box < boxes)
            box = jnp.where(inside, box, 0)
            expand(height, box, inside, chain[slot * rank : (slot + 1) * rank])

    rank = tlow_buf.shape[1]
    rows = lax.broadcasted_iota(jnp.int32, (rank, rank), 0)
    columns = lax.broadcasted_iota(jnp.int32, (rank, rank), 1)
    unit = jnp.where(rows == columns, 1.0, 0.0).astype(BF16)
    ways = [unit]
    for height in range(low_levels - 2, -1, -1):
        following = []
        for box in range(counts[height]):
            way = ways[box // 2]
            moved = dot(way, tlow_buf[starts[height] + box], transposed=True)
            if height == low_levels - 2:
                moved = moved.astype(BF16)
            else:
                moved = stacked(moved if way.shape[0] == rank else folded(moved))
            following.append(moved)
        ways = following
    for leaf in range(leaves):
        moved = dot(ways[leaf], basis_buf[leaf])
        leaf_ways[leaf] = stacked(moved if ways[leaf].shape[0] == rank else folded(moved))

    @pl.when(has_left)
    def _():
        to_right.wait_recv()

    @pl.when(has_right)
    def _():
        to_left.wait_recv()

    vec_buf[pl.ds(0, RIM)] = rim_in[0, pl.ds(0, RIM)]
    vec_buf[pl.ds(RIM + leaves, RIM)] = rim_in[1, pl.ds(0, RIM)]
    at = RIM
    for buf, count, rim in zip(level_bufs, counts, rims):
        buf[pl.ds(0, rim)] = unpacked(rim_in[0, pl.ds(at, rim)])
        buf[pl.ds(rim + count, rim)] = unpacked(rim_in[1, pl.ds(at, rim)])
        at += rim

    near_base = device * leaves - RIM

    def near_step(leaf, carry):
        beside = []
        for slot in range(k_near):
            spot = jnp.where(
                near_mask[slot, leaf] != 0,
                near_list[slot, leaf] - near_base,
                leaves + 2 * RIM,
            )
            beside.append(vec_buf[spot])
        blocks = near_buf[leaf]
        near_acc[leaf] = dot(
            jnp.concatenate(beside, axis=-1),
            blocks.reshape(blocks.shape[0] * blocks.shape[1], blocks.shape[2]),
        )
        return carry

    lax.fori_loop(0, leaves, near_step, 0, unroll=True)

    for height in range(low_levels - 1):
        buf = level_bufs[height]
        far_base = device * counts[height] - rims[height]
        zero_spot = buf.shape[0] - 1

        def far_step(box, carry, buf=buf, far_base=far_base, zero_spot=zero_spot, height=height):
            row = starts[height] + box
            total = None
            for slot in range(k_far):
                spot = jnp.where(
                    far_mask[slot, row] != 0, far_list[slot, row] - far_base, zero_spot
                )
                term = dot(buf[spot], clow_buf[row, slot])
                total = term if total is None else total + term
            far_acc[row] = folded(total)
            return carry

        lax.fori_loop(0, counts[height], far_step, 0, unroll=True)

    expanded = None
    for height in range(low_levels - 2, -1, -1):
        count = counts[height]
        own = far_acc[pl.ds(starts[height], count)]
        if expanded is not None:
            spread = stacked(expanded)
            spread = jnp.broadcast_to(spread[:, None], (count // 2, 2) + spread.shape[1:])
            spread = spread.reshape((count,) + spread.shape[2:])
            mats = tlow_buf[pl.ds(starts[height], count)]
            own = own + folded(bdot(spread, mats, transposed=True))
        expanded = own
    near_acc[...] = near_acc[...] + folded(bdot(stacked(expanded), basis_buf[...]))

    arrived = roots.at[pl.ds(0, tree_devs - 1)]
    pltpu.make_async_copy(arrived, arrived, root_recv).wait()
    total = None
    for first in range(0, len(sources), 8):
        group = range(first, min(first + 8, len(sources)))
        term = dot(
            jnp.concatenate([roots[sources[at]] for at in group], axis=-1),
            jnp.concatenate([doubled(path_buf[at]) for at in group], axis=-2),
        )
        total = term if total is None else total + term
    downward = stacked(twin(total))
    for leaf in range(leaves):
        out[leaf] = (near_acc[leaf] + folded(dot(downward, leaf_ways[leaf]))).astype(out.dtype)

    sent = roots.at[pl.ds(0, tree_devs - 1)]
    pltpu.make_async_copy(sent, sent, root_send).wait()

    @pl.when(has_right)
    def _():
        to_right.wait_send()

    @pl.when(has_left)
    def _():
        to_left.wait_send()


def per_device(
    vectors,
    leaf_basis,
    near_blocks,
    near_list,
    near_mask,
    transfer_low,
    coupling_low,
    far_list,
    far_mask,
    transfer_top,
    coupling_top,
):
    tree_devs = lax.axis_size(("leaf", "sub"))
    num_sub = lax.axis_size("sub")
    leaves, num_vectors, points = vectors.shape
    rank = leaf_basis.shape[1]
    k_near = near_blocks.shape[1]
    k_far = coupling_low.shape[1]
    low_levels = leaves.bit_length()
    top_used = max(tree_devs.bit_length() - 3, 0)
    counts = [leaves >> height for height in range(low_levels - 1)]
    boxes = [
        pltpu.VMEM((count + 2 * min(RIM, count) + 1, 2 * num_vectors, rank), BF16)
        for count in counts
    ]
    rim_boxes = RIM + sum(min(RIM, count) for count in counts)
    paths = k_far * sum(1 << height for height in range(top_used + 1))
    scratch = [
        pltpu.SMEM(near_list.shape[::-1], jnp.int32),
        pltpu.SMEM(near_list.shape[::-1], jnp.int32),
        pltpu.SMEM(far_list.shape[::-1], jnp.int32),
        pltpu.SMEM(far_list.shape[::-1], jnp.int32),
        pltpu.VMEM((leaves + 2 * RIM + 1, num_vectors, points), BF16),
        pltpu.VMEM(leaf_basis.shape, BF16),
        pltpu.VMEM(near_blocks.shape, BF16),
        pltpu.VMEM(transfer_low.shape, BF16),
        pltpu.VMEM(coupling_low.shape, BF16),
        pltpu.VMEM(transfer_top.shape, BF16),
        pltpu.VMEM((top_used,) + coupling_top.shape[1:], BF16),
        pltpu.VMEM(vectors.shape, F32),
        pltpu.VMEM((coupling_low.shape[0], num_vectors, rank), F32),
        pltpu.VMEM((tree_devs + 1, num_vectors, 2 * rank), BF16),
        *boxes,
        pltpu.VMEM((2, rim_boxes, num_vectors, points), BF16),
        pltpu.VMEM((2, rim_boxes, num_vectors, points), BF16),
        pltpu.VMEM((paths, rank, 2 * rank), BF16),
        pltpu.VMEM((leaves, 2 * rank, points), BF16),
        pltpu.SemaphoreType.DMA((10 + top_used,)),
        pltpu.SemaphoreType.DMA((2,)),
        pltpu.SemaphoreType.DMA((2,)),
        pltpu.SemaphoreType.DMA,
        pltpu.SemaphoreType.DMA,
    ]
    sizes = (leaves, low_levels, tree_devs, num_sub, top_used, k_near, k_far)
    return pl.pallas_call(
        functools.partial(kernel, sizes),
        out_shape=pltpu.VMEM(vectors.shape, BF16),
        in_specs=[pl.BlockSpec(memory_space=pltpu.HBM)] * 11,
        out_specs=pl.BlockSpec(memory_space=pltpu.VMEM),
        scratch_shapes=scratch,
        compiler_params=pltpu.CompilerParams(
            collective_id=0, has_side_effects=True, vmem_limit_bytes=60 * 1024 * 1024
        ),
    )(
        near_list.T,
        near_mask.T,
        far_list.T,
        far_mask.T,
        vectors,
        leaf_basis,
        near_blocks,
        transfer_low,
        coupling_low,
        transfer_top,
        coupling_top,
    )


def solution(mesh):
    in_specs = (
        P(("copies", "leaf", "sub"), None, None),
        P(("copies", "leaf", "sub"), None, None),
        P(("copies", "leaf", "sub"), None, None, None),
        P(("leaf", "sub"), None),
        P(("leaf", "sub"), None),
        P(("copies", "leaf", "sub"), None, None),
        P(("copies", "leaf", "sub"), None, None, None),
        P(("leaf", "sub"), None),
        P(("leaf", "sub"), None),
        P("copies", None, None),
        P("copies", None, None, None),
    )
    out_specs = P(("copies", "leaf", "sub"), None, None)
    return jax.shard_map(
        per_device, mesh=mesh, in_specs=in_specs, out_specs=out_specs, check_vma=False
    )
```

```python
import functools

import jax
import jax.numpy as jnp
from jax import lax
from jax.experimental import pallas as pl
from jax.experimental.pallas import tpu as pltpu
from jax.sharding import PartitionSpec as P

RIM = 2
MESH = pl.DeviceIdType.MESH
F32 = jnp.float32
BF16 = jnp.bfloat16


def bdot(left, right, transposed=False):
    contract = 2 if transposed else 1
    return lax.dot_general(
        left, right, (((2,), (contract,)), ((0,), (0,))), preferred_element_type=F32
    )


def split(value):
    high = value.astype(BF16)
    low = (value - high.astype(F32)).astype(BF16)
    return high, low


def stacked(value):
    return jnp.concatenate(split(value), axis=-2)


def folded(value):
    half = value.shape[-2] // 2
    return value[..., :half, :] + value[..., half:, :]


def packed(value):
    high = value.astype(BF16).astype(F32)
    return jnp.concatenate([high, value - high], axis=-1).astype(BF16)


def packed_twin(value):
    high = value.astype(BF16).astype(F32)
    lanes = lax.broadcasted_iota(jnp.int32, value.shape, value.ndim - 1)
    return jnp.where(lanes < value.shape[-1] // 2, high, value - high).astype(BF16)


def unpacked(pair):
    rank = pair.shape[-1] // 2
    return jnp.concatenate([pair[..., :rank], pair[..., rank:]], axis=-2)


def twin(value):
    return value + pltpu.roll(value, value.shape[-1] // 2, value.ndim - 1)


def doubled(matrix):
    return jnp.concatenate([matrix, matrix], axis=-2)


def dot(left, right, transposed=False):
    contract = 1 if transposed else 0
    return lax.dot_general(
        left, right, (((1,), (contract,)), ((), ())), preferred_element_type=F32
    )


def kernel(
    sizes,
    near_list_in,
    far_list_in,
    vectors,
    basis,
    near_blocks,
    transfer_low,
    coupling_low,
    transfer_top,
    coupling_top,
    out,
    near_list,
    far_list,
    vec_buf,
    basis_buf,
    near_buf,
    tlow_buf,
    clow_buf,
    ttop_buf,
    ctop_buf,
    near_acc,
    far_acc,
    roots,
    *rest,
):
    leaves, low_levels, tree_devs, num_sub, top_used, k_near, k_far = sizes
    level_bufs = rest[: low_levels - 1]
    rim_out, rim_in, path_buf, leaf_ways = rest[low_levels - 1 : -5]
    local_sem, rim_send, rim_recv, root_send, root_recv = rest[-5:]
    leaf_at = lax.axis_index("leaf")
    device = leaf_at * num_sub + lax.axis_index("sub")
    copy_at = lax.axis_index("copies")

    def place(index):
        return (copy_at, index // num_sub, index % num_sub)

    barrier = pltpu.get_barrier_semaphore()

    def greet(step, carry):
        pl.semaphore_signal(
            barrier, inc=1, device_id=place((device + step) % tree_devs), device_id_type=MESH
        )
        return carry

    moves = [
        (vectors, vec_buf.at[pl.ds(RIM, leaves)]),
        (basis, basis_buf),
        (transfer_low, tlow_buf),
        (near_list_in, near_list),
        (near_blocks, near_buf),
        (far_list_in, far_list),
        (coupling_low, clow_buf),
        (transfer_top, ttop_buf),
    ]
    for height in range(1, top_used + 1):
        row = tree_devs - 2 * (tree_devs >> height) + device // (1 << height)
        moves.append((coupling_top.at[row], ctop_buf.at[height - 1]))
    copies = [
        pltpu.make_async_copy(source, target, local_sem.at[at])
        for at, (source, target) in enumerate(moves)
    ]
    for copy in copies[:3]:
        copy.start()
    rim_in[:, pl.ds(0, RIM)] = jnp.zeros((2, RIM) + rim_in.shape[2:], BF16)
    lax.fori_loop(1, tree_devs, greet, 0, unroll=tree_devs <= 16)
    for copy in copies[3:]:
        copy.start()

    starts = [2 * leaves - 2 * (leaves >> height) for height in range(low_levels)]
    counts = [leaves >> height for height in range(low_levels)]
    rims = [min(RIM, count) for count in counts]

    vec_buf[leaves + 2 * RIM] = jnp.zeros(vec_buf.shape[1:], BF16)
    for buf in level_bufs:
        buf[buf.shape[0] - 1] = jnp.zeros(buf.shape[1:], BF16)
    roots[tree_devs] = jnp.zeros(roots.shape[1:], BF16)

    to_right, to_left = [
        pltpu.make_async_remote_copy(
            src_ref=rim_out.at[side],
            dst_ref=rim_in.at[side],
            send_sem=rim_send.at[side],
            recv_sem=rim_recv.at[side],
            device_id=place(device + step),
            device_id_type=MESH,
        )
        for side, step in ((0, 1), (1, -1))
    ]
    has_right = device < tree_devs - 1
    has_left = device > 0

    copies[0].wait()
    copies[1].wait()
    coefs = bdot(vec_buf[pl.ds(RIM, leaves)], basis_buf[...], transposed=True)
    level_coefs = [coefs]
    pieces = []
    copies[2].wait()
    for height in range(1, low_levels):
        below = counts[height - 1]
        pieces.append(stacked(coefs))
        moved = folded(bdot(pieces[-1], tlow_buf[pl.ds(starts[height - 1], below)]))
        moved = moved.reshape((below // 2, 2) + moved.shape[1:])
        coefs = moved[:, 0] + moved[:, 1]
        level_coefs.append(coefs)
    roots[device] = packed(coefs[0])
    pl.semaphore_wait(barrier, tree_devs - 1)

    def send_root(step, carry):
        pltpu.make_async_remote_copy(
            src_ref=roots.at[device],
            dst_ref=roots.at[device],
            send_sem=root_send,
            recv_sem=root_recv,
            device_id=place((device + step) % tree_devs),
            device_id_type=MESH,
        ).start()
        return carry

    lax.fori_loop(1, tree_devs, send_root, 0, unroll=tree_devs <= 16)

    rim_out[0, pl.ds(0, RIM)] = vec_buf[pl.ds(leaves, RIM)]
    rim_out[1, pl.ds(0, RIM)] = vec_buf[pl.ds(RIM, RIM)]
    at = RIM
    for count, rim, coefs in zip(counts, rims, level_coefs[:-1]):
        rim_out[0, pl.ds(at, rim)] = packed(coefs[count - rim :])
        rim_out[1, pl.ds(at, rim)] = packed(coefs[:rim])
        at += rim

    @pl.when(has_right)
    def _():
        to_right.start()

    @pl.when(has_left)
    def _():
        to_left.start()

    for height in range(low_levels - 1):
        level_bufs[height][pl.ds(rims[height], counts[height])] = pieces[height]
    for copy in copies[3:]:
        copy.wait()

    def first_of(height):
        return 2 * tree_devs - 2 * (tree_devs >> height)

    sources = []
    root_row = starts[low_levels - 1]
    for slot in range(k_far):
        spot = far_list[slot, root_row]
        spot = jnp.where(spot == device, tree_devs, spot)
        near_path = clow_buf[root_row, slot]
        path_buf[len(sources)] = jnp.concatenate([near_path, jnp.zeros_like(near_path)], axis=-1)
        sources.append(spot)

    def expand(height, box, inside, matrix):
        matrix = packed_twin(matrix)
        if height == 0:
            path_buf[len(sources)] = matrix
            sources.append(jnp.where(inside, box, tree_devs))
            return
        mats = ttop_buf[pl.ds(first_of(height - 1) + 2 * box, 2)]
        mats = mats.reshape(2 * mats.shape[1], mats.shape[2])
        both = twin(dot(mats, matrix))
        rank = matrix.shape[0]
        expand(height - 1, 2 * box, inside, both[:rank])
        expand(height - 1, 2 * box + 1, inside, both[rank:])

    for height in range(1, top_used + 1):
        node = device // (1 << height)
        boxes = tree_devs >> height
        chain = ctop_buf[height - 1]
        rank = chain.shape[1]
        chain = chain.reshape(chain.shape[0] * rank, chain.shape[2])
        for step in range(height - 1, -1, -1):
            matrix = ttop_buf[first_of(step) + device // (1 << step)]
            if step == 0:
                matrix = doubled(matrix)
            if step == height - 1:
                chain = dot(chain, matrix, transposed=True)
            else:
                chain = folded(dot(stacked(chain), matrix, transposed=True))
        odd = node % 2
        for slot, (even_step, odd_step) in enumerate(((-2, -3), (2, -2), (3, 2))):
            box = node + jnp.where(odd == 1, odd_step, even_step)
            inside = (box >= 0) & (box < boxes)
            box = jnp.where(inside, box, 0)
            expand(height, box, inside, chain[slot * rank : (slot + 1) * rank])

    rank = tlow_buf.shape[1]
    rows = lax.broadcasted_iota(jnp.int32, (rank, rank), 0)
    columns = lax.broadcasted_iota(jnp.int32, (rank, rank), 1)
    unit = jnp.where(rows == columns, 1.0, 0.0).astype(BF16)
    ways = [unit]
    for height in range(low_levels - 2, -1, -1):
        following = []
        for box in range(counts[height]):
            way = ways[box // 2]
            moved = dot(way, tlow_buf[starts[height] + box], transposed=True)
            if height == low_levels - 2:
                moved = moved.astype(BF16)
            else:
                moved = stacked(moved if way.shape[0] == rank else folded(moved))
            following.append(moved)
        ways = following
    for leaf in range(leaves):
        moved = dot(ways[leaf], basis_buf[leaf])
        leaf_ways[leaf] = stacked(moved if ways[leaf].shape[0] == rank else folded(moved))

    @pl.when(has_left)
    def _():
        to_right.wait_recv()

    @pl.when(has_right)
    def _():
        to_left.wait_recv()

    vec_buf[pl.ds(0, RIM)] = rim_in[0, pl.ds(0, RIM)]
    vec_buf[pl.ds(RIM + leaves, RIM)] = rim_in[1, pl.ds(0, RIM)]
    at = RIM
    for buf, count, rim in zip(level_bufs, counts, rims):
        buf[pl.ds(0, rim)] = unpacked(rim_in[0, pl.ds(at, rim)])
        buf[pl.ds(rim + count, rim)] = unpacked(rim_in[1, pl.ds(at, rim)])
        at += rim

    near_base = device * leaves - RIM

    def near_step(leaf, carry):
        beside = []
        for step in (-1, 0, 1):
            beside.append(vec_buf[RIM + leaf + step])
        for slot in range(3, k_near):
            spot = jnp.maximum(near_list[slot, leaf] - near_base, 0)
            beside.append(vec_buf[jnp.where(spot == RIM + leaf, leaves + 2 * RIM, spot)])
        blocks = near_buf[leaf]
        near_acc[leaf] = dot(
            jnp.concatenate(beside, axis=-1),
            blocks.reshape(blocks.shape[0] * blocks.shape[1], blocks.shape[2]),
        )
        return carry

    lax.fori_loop(0, leaves, near_step, 0, unroll=True)

    for height in range(low_levels - 1):
        buf = level_bufs[height]
        far_base = device * counts[height] - rims[height]
        zero_spot = buf.shape[0] - 1

        def far_step(box, carry, buf=buf, far_base=far_base, zero_spot=zero_spot, height=height):
            row = starts[height] + box
            total = None
            for slot in range(k_far):
                spot = jnp.maximum(far_list[slot, row] - far_base, 0)
                spot = jnp.where(spot == rims[height] + box, zero_spot, spot)
                term = dot(buf[spot], clow_buf[row, slot])
                total = term if total is None else total + term
            far_acc[row] = folded(total)
            return carry

        lax.fori_loop(0, counts[height], far_step, 0, unroll=True)

    expanded = None
    for height in range(low_levels - 2, -1, -1):
        count = counts[height]
        own = far_acc[pl.ds(starts[height], count)]
        if expanded is not None:
            spread = stacked(expanded)
            spread = jnp.broadcast_to(spread[:, None], (count // 2, 2) + spread.shape[1:])
            spread = spread.reshape((count,) + spread.shape[2:])
            mats = tlow_buf[pl.ds(starts[height], count)]
            own = own + folded(bdot(spread, mats, transposed=True))
        expanded = own
    near_acc[...] = near_acc[...] + folded(bdot(stacked(expanded), basis_buf[...]))

    arrived = roots.at[pl.ds(0, tree_devs - 1)]
    pltpu.make_async_copy(arrived, arrived, root_recv).wait()
    total = None
    for first in range(0, len(sources), 8):
        group = range(first, min(first + 8, len(sources)))
        term = dot(
            jnp.concatenate([roots[sources[at]] for at in group], axis=-1),
            jnp.concatenate([doubled(path_buf[at]) for at in group], axis=-2),
        )
        total = term if total is None else total + term
    downward = stacked(twin(total))
    for leaf in range(leaves):
        out[leaf] = (near_acc[leaf] + folded(dot(downward, leaf_ways[leaf]))).astype(out.dtype)

    sent = roots.at[pl.ds(0, tree_devs - 1)]
    pltpu.make_async_copy(sent, sent, root_send).wait()

    @pl.when(has_right)
    def _():
        to_right.wait_send()

    @pl.when(has_left)
    def _():
        to_left.wait_send()


def per_device(
    vectors,
    leaf_basis,
    near_blocks,
    near_list,
    near_mask,
    transfer_low,
    coupling_low,
    far_list,
    far_mask,
    transfer_top,
    coupling_top,
):
    tree_devs = lax.axis_size(("leaf", "sub"))
    num_sub = lax.axis_size("sub")
    leaves, num_vectors, points = vectors.shape
    rank = leaf_basis.shape[1]
    k_near = near_blocks.shape[1]
    k_far = coupling_low.shape[1]
    low_levels = leaves.bit_length()
    top_used = max(tree_devs.bit_length() - 3, 0)
    counts = [leaves >> height for height in range(low_levels - 1)]
    boxes = [
        pltpu.VMEM((count + 2 * min(RIM, count) + 1, 2 * num_vectors, rank), BF16)
        for count in counts
    ]
    rim_boxes = RIM + sum(min(RIM, count) for count in counts)
    paths = k_far * sum(1 << height for height in range(top_used + 1))
    scratch = [
        pltpu.SMEM(near_list.shape[::-1], jnp.int32),
        pltpu.SMEM(far_list.shape[::-1], jnp.int32),
        pltpu.VMEM((leaves + 2 * RIM + 1, num_vectors, points), BF16),
        pltpu.VMEM(leaf_basis.shape, BF16),
        pltpu.VMEM(near_blocks.shape, BF16),
        pltpu.VMEM(transfer_low.shape, BF16),
        pltpu.VMEM(coupling_low.shape, BF16),
        pltpu.VMEM(transfer_top.shape, BF16),
        pltpu.VMEM((top_used,) + coupling_top.shape[1:], BF16),
        pltpu.VMEM(vectors.shape, F32),
        pltpu.VMEM((coupling_low.shape[0], num_vectors, rank), F32),
        pltpu.VMEM((tree_devs + 1, num_vectors, 2 * rank), BF16),
        *boxes,
        pltpu.VMEM((2, rim_boxes, num_vectors, points), BF16),
        pltpu.VMEM((2, rim_boxes, num_vectors, points), BF16),
        pltpu.VMEM((paths, rank, 2 * rank), BF16),
        pltpu.VMEM((leaves, 2 * rank, points), BF16),
        pltpu.SemaphoreType.DMA((8 + top_used,)),
        pltpu.SemaphoreType.DMA((2,)),
        pltpu.SemaphoreType.DMA((2,)),
        pltpu.SemaphoreType.DMA,
        pltpu.SemaphoreType.DMA,
    ]
    sizes = (leaves, low_levels, tree_devs, num_sub, top_used, k_near, k_far)
    return pl.pallas_call(
        functools.partial(kernel, sizes),
        out_shape=pltpu.VMEM(vectors.shape, BF16),
        in_specs=[pl.BlockSpec(memory_space=pltpu.HBM)] * 9,
        out_specs=pl.BlockSpec(memory_space=pltpu.VMEM),
        scratch_shapes=scratch,
        compiler_params=pltpu.CompilerParams(
            collective_id=0, has_side_effects=True, vmem_limit_bytes=60 * 1024 * 1024
        ),
    )(
        near_list.T,
        far_list.T,
        vectors,
        leaf_basis,
        near_blocks,
        transfer_low,
        coupling_low,
        transfer_top,
        coupling_top,
    )


def solution(mesh):
    in_specs = (
        P(("copies", "leaf", "sub"), None, None),
        P(("copies", "leaf", "sub"), None, None),
        P(("copies", "leaf", "sub"), None, None, None),
        P(("leaf", "sub"), None),
        P(("leaf", "sub"), None),
        P(("copies", "leaf", "sub"), None, None),
        P(("copies", "leaf", "sub"), None, None, None),
        P(("leaf", "sub"), None),
        P(("leaf", "sub"), None),
        P("copies", None, None),
        P("copies", None, None, None),
    )
    out_specs = P(("copies", "leaf", "sub"), None, None)
    return jax.shard_map(
        per_device, mesh=mesh, in_specs=in_specs, out_specs=out_specs, check_vma=False
    )
```
